128 devices in a mesh: dp: 4 (over x), tp: 32 (over z, y, core).
Axes of the slice: x: 4, y: 4, z: 4, core: 2. Of those that a mesh axis runs over, the one named last changes fastest.
Arguments:
- hidden: bfloat16 [8192, 14784], P(('dp', 'tp')), may hold values from -6 to 6
- draft_row_client: int32 [8192], P(('dp', 'tp')), may hold values from 0 to 255, as said below
- client_rank_bin: int32 [256], replicated, may hold values from 8 to 256, as said below
- client_device: int32 [256], replicated, may hold values from 0 to 127, as said below
- down_weight: bfloat16 [14784, 8192], P('tp'), may hold values from -0.046875 to 0.046875
- packed_down_factors: bfloat16 [14784, 40960], P(None, ('dp', 'tp')), may hold values from -0.046875 to 0.046875
- packed_up_factors: bfloat16 [40960, 8192], P(('dp', 'tp')), may hold values from -0.75 to 0.75
Outputs:
- projected: bfloat16 [8192, 8192], P(('dp', 'tp'))
The draws below stay inside these ranges and needn't reach their ends.
Inputs may be any that keep to these rules, and one draw needn't show every extreme that they name: `client_device`: each device holds exactly two tenants. `client_rank_bin`: ranks are powers of two; the two tenants of one device have ranks summing to at most 320, and some device's sum is exactly 320; a device's adapters are packed from its first column in increasing tenant order. `draft_row_client`: of the rows of one device, at most 24 belong to tenants whose device lies in any one dp group; of all rows on the devices of one tp index whose tenants lie in one dp group, at most 3 belong to the tenants of any one device of that group.
All inputs are finite; a program needn't handle non-finite values.
Results may differ from the reference program's by a relative error of at most 0.0065.
Values may be sent and summed in bfloat16 or wider, within the bound.
A program may use at most 448 MiB of HBM per device.

```python
import jax
import jax.numpy as jnp
from jax import lax

MODEL_WIDTH = 8192
WINDOW_HIDDEN = 14784
RANK_COLUMNS = 320
TOK_DEV = 64
TOKENS = 8192
TENANTS = 256
GROUP_CAP = 24
OWNER_CAP = 3
N_DP = 4
N_TP = 32
DEVICES = 128


def shared_layout(key):
    unit_table = jnp.array([[32, 8], [16, 16], [16, 8], [8, 8], [32, 4], [4, 2], [16, 1], [8, 4], [2, 1], [32, 1]], jnp.int32)
    key_pick, key_full, key_small, key_seat = jax.random.split(key, 4)
    pattern = jax.random.randint(key_pick, (DEVICES,), 0, 10)
    full_device = jax.random.randint(key_full, (), 0, DEVICES)
    small_device = (full_device + 1 + jax.random.randint(key_small, (), 0, DEVICES - 1)) % DEVICES
    pattern = pattern.at[full_device].set(0).at[small_device].set(8)
    pair_ranks = unit_table[pattern] * (RANK_COLUMNS // 40)
    seat = jax.random.permutation(key_seat, TENANTS).astype(jnp.int32)
    return ((seat // 2).astype(jnp.int32), pair_ranks.reshape(-1)[seat].astype(jnp.int32), seat)


def draw_client_device(key, part):
    device_of, rank_of, seat = shared_layout(key)
    return device_of


def draw_client_rank_bin(key, part):
    device_of, rank_of, seat = shared_layout(key)
    return rank_of


def draw_draft_row_client(key, part):
    device_of, rank_of, seat = shared_layout(key)
    key = jax.random.fold_in(key, 11)
    key_hot, key_turn, key_owner, key_perm, key_bit, key_shuffle = jax.random.split(key, 6)
    occupant = jnp.argsort(seat).astype(jnp.int32)
    hot_group = jax.random.randint(key_hot, (N_TP,), 0, N_DP)
    turn = jax.random.randint(key_turn, (N_TP, N_DP), 0, 3)
    groups = jnp.arange(N_DP, dtype=jnp.int32)
    relative = (groups[None, None, :] - hot_group[:, None, None] - 1) % N_DP
    share = jnp.array([2, 2, 1], jnp.int32) * (TOK_DEV // 8)
    other = share[(relative + turn[:, :, None]) % 3]
    counts = jnp.where(groups[None, None, :] == hot_group[:, None, None], GROUP_CAP, other)
    first = jnp.cumsum(counts, axis=1) - counts
    entries = jnp.arange(GROUP_CAP, dtype=jnp.int32)
    order_in = first[..., None] + entries
    occupied = entries < counts[..., None]
    spread = max(N_DP * GROUP_CAP - OWNER_CAP, 1)
    seat_rank = jnp.where(order_in < OWNER_CAP, 0, 1 + (order_in - OWNER_CAP) * (N_TP - 1) // spread)
    seat_rank = jnp.minimum(seat_rank, N_TP - 1)
    hot_owner = jax.random.randint(key_owner, (N_DP,), 0, N_TP)
    scores = jax.random.randint(key_perm, (N_DP, N_TP, N_TP), 0, 1 << 20) * N_TP + jnp.arange(N_TP, dtype=jnp.int32)
    base_perm = jnp.argsort(scores, axis=-1).astype(jnp.int32)
    owner_perm = (base_perm - base_perm[..., :1] + hot_owner[:, None, None]) % N_TP
    tp_ids = jnp.arange(N_TP, dtype=jnp.int32)
    owner_tp = owner_perm[groups[None, None, :, None], tp_ids[:, None, None, None], seat_rank]
    device = groups[None, None, :, None] * N_TP + owner_tp
    pick_bit = jax.random.randint(key_bit, (N_TP, N_DP, N_DP, GROUP_CAP), 0, 2)
    tenant = occupant[2 * device + pick_bit]
    flat_tenant = tenant.reshape(N_TP, N_DP, N_DP * GROUP_CAP)
    flat_live = occupied.reshape(N_TP, N_DP, N_DP * GROUP_CAP)
    chosen = jnp.argsort(jnp.where(flat_live, 0, 1), axis=-1)[..., :TOK_DEV]
    picked = jnp.take_along_axis(flat_tenant, chosen, axis=-1)
    mixing = jax.random.randint(key_shuffle, (N_TP, N_DP, TOK_DEV), 0, 1 << 20) * TOK_DEV + jnp.arange(TOK_DEV, dtype=jnp.int32)
    shuffle = jnp.argsort(mixing, axis=-1)
    picked = jnp.take_along_axis(picked, shuffle, axis=-1)
    return jnp.transpose(picked, (1, 0, 2)).reshape(TOKENS).astype(jnp.int32)


def shard_levels(rng, shape, pieces, least, high):
    gain, own = 1.0, jax.random.fold_in(rng, 6)
    for dim, shards_of in pieces:
        heights = jnp.exp(jax.random.uniform(jax.random.fold_in(own, dim), (shards_of,), jnp.float32, least / len(pieces), high / len(pieces)))
        gain = gain * jnp.repeat(heights, shape[dim] // shards_of).reshape([-1 if axis == dim else 1 for axis in range(len(shape))])
    return gain


def gaussian(own_key, shape, scale, limit, shards=(), held_as=jnp.bfloat16):
    values = scale * jax.random.normal(own_key, shape, jnp.float32)
    if shards:
        values = values * shard_levels(own_key, shape, shards, -0.22, 0.18)
    return jnp.clip(values, -limit, limit).astype(held_as)


def setup_inputs(seed: int = 0) -> dict:
    key_list = jax.random.split(jax.random.key(seed), 8)
    hidden = gaussian(key_list[0], (TOKENS, WINDOW_HIDDEN), 1.0, 6.0, ((0, 128),))
    draft_row_client = draw_draft_row_client(jax.random.fold_in(key_list[7], 71), 0)
    client_rank_bin = draw_client_rank_bin(jax.random.fold_in(key_list[7], 71), 0)
    client_device = draw_client_device(jax.random.fold_in(key_list[7], 71), 0)
    down_weight = gaussian(key_list[4], (WINDOW_HIDDEN, MODEL_WIDTH), WINDOW_HIDDEN ** -0.5, 0.046875, ((0, 32),))
    packed_down_factors = gaussian(key_list[5], (WINDOW_HIDDEN, RANK_COLUMNS * DEVICES), WINDOW_HIDDEN ** -0.5, 0.046875, ((1, 128),))
    packed_up_factors = gaussian(key_list[6], (RANK_COLUMNS * DEVICES, MODEL_WIDTH), 64 ** -0.5, 0.75, ((0, 128),))
    return dict(hidden=hidden, draft_row_client=draft_row_client, client_rank_bin=client_rank_bin, client_device=client_device, down_weight=down_weight, packed_down_factors=packed_down_factors, packed_up_factors=packed_up_factors)


adapter_scale_fn = 4.0

def adapter_tables(client_rank_bin, client_device):
    client_indices = jnp.arange(client_rank_bin.shape[0], dtype=jnp.int32)
    earlier = (client_device[:, None] == client_device[None, :]) & (client_indices[None, :] < client_indices[:, None])
    column_offset = lax.optimization_barrier(jnp.sum(jnp.where(earlier, client_rank_bin[None, :], 0), axis=1)).astype(jnp.int32)
    adapter_scale = adapter_scale_fn / jnp.sqrt(client_rank_bin.astype(jnp.float32))
    return (column_offset, adapter_scale)

def reference(hidden, draft_row_client, client_rank_bin, client_device, down_weight, packed_down_factors, packed_up_factors):
    column_offset, adapter_scale = adapter_tables(client_rank_bin, client_device)
    column_span = jnp.arange(RANK_COLUMNS, dtype=jnp.int32)

    def one_row(item):
        row, tenant = item
        device = client_device[tenant]
        start_position = (device * RANK_COLUMNS).astype(jnp.int32)
        zero_position = jnp.zeros((), jnp.int32)
        down_factor_block = lax.dynamic_slice(packed_down_factors, (zero_position, start_position), (WINDOW_HIDDEN, RANK_COLUMNS))
        up_factor_block = lax.dynamic_slice(packed_up_factors, (start_position, zero_position), (RANK_COLUMNS, MODEL_WIDTH))
        projected = jnp.dot(row[None, :], down_factor_block, preferred_element_type=jnp.float32)[0]
        in_range = (column_span >= column_offset[tenant]) & (column_span < column_offset[tenant] + client_rank_bin[tenant])
        rank_space = (jnp.where(in_range, projected, jnp.zeros_like(projected)) * adapter_scale[tenant]).astype(jnp.bfloat16)
        return jnp.dot(rank_space[None, :], up_factor_block, preferred_element_type=jnp.float32)[0]
    adapter = lax.map(one_row, (hidden, draft_row_client))
    base = jnp.dot(hidden, down_weight, preferred_element_type=jnp.float32)
    return (base + adapter).astype(jnp.bfloat16)
```

```python
import jax
import jax.numpy as jnp
from jax import lax
from jax.sharding import PartitionSpec as P

adapter_scale_fn = 4.0


def adapter_tables(client_rank_bin, client_device):
    client_indices = jnp.arange(client_rank_bin.shape[0], dtype=jnp.int32)
    earlier = (client_device[:, None] == client_device[None, :]) & (
        client_indices[None, :] < client_indices[:, None]
    )
    column_offset = jnp.sum(jnp.where(earlier, client_rank_bin[None, :], 0), axis=1)
    adapter_scale = adapter_scale_fn / jnp.sqrt(client_rank_bin.astype(jnp.float32))
    return (column_offset, adapter_scale)


def lookup(client_indices, table_values):
    matches = client_indices[:, None] == jnp.arange(table_values.shape[0], dtype=jnp.int32)[None, :]
    return jnp.sum(
        jnp.where(matches, table_values[None, :], jnp.zeros((), table_values.dtype)), axis=1
    )


def bucket_matrix(bucket_id, occupied, buckets, capacity):
    matches = (bucket_id[:, None] == jnp.arange(buckets, dtype=jnp.int32)[None, :]) & occupied[
        :, None
    ]
    rank_in = jnp.cumsum(matches.astype(jnp.int32), axis=0) - 1
    within = jnp.sum(jnp.where(matches, rank_in, 0), axis=1)
    target = jnp.where(occupied, bucket_id * capacity + within, -1)
    return jnp.arange(buckets * capacity, dtype=jnp.int32)[:, None] == target[None, :]


def adapter_row_block(
    row_span,
    client_indices,
    column_offset,
    client_rank_bin,
    adapter_scale,
    packed_down_factors,
    packed_up_factors,
):
    projected = jnp.dot(row_span, packed_down_factors, preferred_element_type=jnp.float32)
    col_start = lookup(client_indices, column_offset)
    col_count = lookup(client_indices, client_rank_bin)
    row_gain = lookup(client_indices, adapter_scale)
    column_span = jnp.arange(packed_down_factors.shape[1], dtype=jnp.int32)[None, :]
    in_range = (column_span >= col_start[:, None]) & (
        column_span < (col_start + col_count)[:, None]
    )
    rank_space = (jnp.where(in_range, projected, 0.0) * row_gain[:, None]).astype(jnp.bfloat16)
    return jnp.dot(rank_space, packed_up_factors, preferred_element_type=jnp.float32)


def local(
    hidden,
    draft_row_client,
    client_rank_bin,
    client_device,
    down_weight,
    packed_down_factors,
    packed_up_factors,
):
    dp_count = lax.axis_size("dp")
    tp_count = lax.axis_size("tp")
    rows_home = hidden.shape[0]
    width = down_weight.shape[1]
    group_cap = 3 * rows_home // 8
    owner_cap = max(2, (dp_count * group_cap + tp_count - 1) // tp_count)
    slots = dp_count * group_cap
    chips = tp_count // 2
    pairs = [[2 * i, 2 * i + 1] for i in range(chips)]
    plane = [[2 * i + core for i in range(chips)] for core in range(2)]
    weight = lax.all_gather(down_weight, "tp", axis_index_groups=pairs, tiled=True)
    features = lax.all_to_all(
        hidden.reshape(rows_home, chips, -1),
        "tp",
        split_axis=1,
        concat_axis=0,
        axis_index_groups=plane,
        tiled=True,
    ).reshape(chips * rows_home, -1)
    base = lax.psum_scatter(
        jnp.dot(features, weight, preferred_element_type=jnp.float32).astype(jnp.bfloat16),
        "tp",
        scatter_dimension=0,
        axis_index_groups=plane,
        tiled=True,
    )
    column_offset, adapter_scale = adapter_tables(client_rank_bin, client_device)
    home_device = lookup(draft_row_client, client_device)
    home_pick = bucket_matrix(
        home_device // tp_count, jnp.ones((rows_home,), bool), dp_count, group_cap
    )
    packed = jnp.dot(
        home_pick.astype(jnp.bfloat16), hidden, preferred_element_type=jnp.float32
    ).astype(jnp.bfloat16)
    packed_tenant = jnp.sum(jnp.where(home_pick, draft_row_client[None, :] + 1, 0), axis=1) - 1
    group_rows, group_tenant = (
        lax.all_to_all(
            packed.reshape(dp_count, group_cap, -1), "dp", split_axis=0, concat_axis=0, tiled=True
        ),
        lax.all_to_all(
            packed_tenant.reshape(dp_count, group_cap),
            "dp",
            split_axis=0,
            concat_axis=0,
            tiled=True,
        ),
    )
    group_rows = group_rows.reshape(slots, -1)
    group_tenant = group_tenant.reshape(slots)
    occupied = group_tenant >= 0
    group_device = lookup(group_tenant, client_device)
    owner_pick = bucket_matrix(group_device % tp_count, occupied, tp_count, owner_cap)
    owner_rows = jnp.dot(
        owner_pick.astype(jnp.bfloat16), group_rows, preferred_element_type=jnp.float32
    ).astype(jnp.bfloat16)
    owner_tenant = jnp.sum(jnp.where(owner_pick, group_tenant[None, :] + 1, 0), axis=1) - 1
    owner_spot = jnp.sum(
        jnp.where(owner_pick, jnp.arange(slots, dtype=jnp.int32)[None, :], 0), axis=1
    )
    got_rows, got_tenant, got_spot = (
        lax.all_to_all(
            owner_rows.reshape(tp_count, owner_cap, -1),
            "tp",
            split_axis=0,
            concat_axis=0,
            tiled=True,
        ),
        lax.all_to_all(
            owner_tenant.reshape(tp_count, owner_cap), "tp", split_axis=0, concat_axis=0, tiled=True
        ),
        lax.all_to_all(
            owner_spot.reshape(tp_count, owner_cap), "tp", split_axis=0, concat_axis=0, tiled=True
        ),
    )
    adapter_out = adapter_row_block(
        got_rows.reshape(tp_count * owner_cap, -1),
        got_tenant.reshape(-1),
        column_offset,
        client_rank_bin,
        adapter_scale,
        packed_down_factors,
        packed_up_factors,
    )
    arrived = lax.all_to_all(
        adapter_out.reshape(tp_count, owner_cap, width).astype(jnp.bfloat16),
        "tp",
        split_axis=0,
        concat_axis=0,
        tiled=True,
    )
    group_out = jnp.dot(
        owner_pick.astype(jnp.bfloat16).T,
        arrived.reshape(tp_count * owner_cap, width),
        preferred_element_type=jnp.float32,
    ).astype(jnp.bfloat16)
    home_rows = lax.all_to_all(
        group_out.reshape(dp_count, group_cap, width), "dp", split_axis=0, concat_axis=0, tiled=True
    ).reshape(slots, width)
    adapter = jnp.dot(
        home_pick.astype(jnp.bfloat16).T, home_rows, preferred_element_type=jnp.float32
    )
    return (base.astype(jnp.float32) + adapter).astype(jnp.bfloat16)


def solution(mesh):
    placed = (
        P(("dp", "tp"), None),
        P(("dp", "tp")),
        P(),
        P(),
        P("tp", None),
        P(None, ("dp", "tp")),
        P(("dp", "tp"), None),
    )
    return jax.shard_map(
        local, mesh=mesh, in_specs=placed, out_specs=P(("dp", "tp"), None), check_vma=False
    )
```

```python
import functools

import jax
import jax.numpy as jnp
from jax import lax
from jax.experimental import pallas as pl
from jax.experimental.pallas import tpu as pltpu
from jax.sharding import PartitionSpec as P

MESH = pl.DeviceIdType.MESH
BF16 = jnp.bfloat16
F32 = jnp.float32
adapter_scale_fn = 4.0

RING = 4
CHIPS = RING * RING
TP = 2 * CHIPS
HOME = 64
CAP = 24
OWN = 3
SLOTS = RING * CAP
LANES = 512
TILE = 512
SLAB_ROWS = TP
OUT_ROWS = 16


def prefix_count(match):
    n = match.shape[0]
    order = jnp.arange(n, dtype=jnp.int32)
    tri = (order[None, :] <= order[:, None]).astype(BF16)
    return jnp.dot(tri, match.astype(BF16), preferred_element_type=F32).astype(jnp.int32)


def lookup(index, table):
    hit = index[:, None] == jnp.arange(table.shape[0], dtype=jnp.int32)[None, :]
    return jnp.sum(jnp.where(hit, table[None, :], 0), axis=1)


def place(target, value, size):
    hit = jnp.arange(size, dtype=jnp.int32)[:, None] == target[None, :]
    return jnp.sum(jnp.where(hit, value[None, :], 0), axis=1)


def routing(draft_row_client, client_rank_bin, client_device):
    x, t = lax.axis_index("dp"), lax.axis_index("tp")
    slots = jnp.arange(SLOTS, dtype=jnp.int32)

    def send(values, axis, parts):
        return lax.all_to_all(
            values.reshape(parts, SLOTS // parts), axis, split_axis=0, concat_axis=0, tiled=True
        ).reshape(SLOTS)

    group = lookup(draft_row_client, client_device) // TP
    hit = group[:, None] == jnp.arange(RING, dtype=jnp.int32)[None, :]
    rank = jnp.sum(jnp.where(hit, prefix_count(hit) - 1, 0), axis=1)
    slot_of_row = group * CAP + rank
    home_index = place(slot_of_row, jnp.arange(HOME, dtype=jnp.int32), SLOTS)

    tenant = send(place(slot_of_row, draft_row_client + 1, SLOTS), "dp", RING) - 1
    position = lookup(tenant, client_device) % TP
    hit = (position[:, None] == jnp.arange(TP, dtype=jnp.int32)[None, :]) & (tenant >= 0)[:, None]
    rank = jnp.sum(jnp.where(hit, prefix_count(hit) - 1, 0), axis=1)
    owner = jnp.where(tenant >= 0, position * OWN + rank, -1)
    owner_index = place(owner, slots, SLOTS)
    back_index = jnp.maximum(owner, 0)

    tenant = send(place(owner, tenant + 1, SLOTS), "tp", TP) - 1
    tenant_id = jnp.arange(client_device.shape[0], dtype=jnp.int32)
    first = jnp.min(jnp.where(client_device == x * TP + t, tenant_id, client_device.shape[0]))
    first_rank = jnp.sum(jnp.where(tenant_id == first, client_rank_bin, 0))
    start = jnp.where(tenant == first, 0, first_rank)
    count = lookup(tenant, client_rank_bin)
    gain = jnp.where(
        count > 0, adapter_scale_fn / jnp.sqrt(jnp.maximum(count, 1).astype(F32)), 0.0
    )
    return home_index, owner_index, back_index, slot_of_row, start, count, gain


def body(
    index,
    gains,
    rows_in,
    slabs_in,
    weight_in,
    down_in,
    down_tail,
    up_in,
    out,
    fin_hbm,
    xrecv,
    weight,
    packed,
    gathered,
    owned,
    wide,
    down,
    up,
    back_out,
    back_in,
    home_out,
    home_in,
    parts,
    relay,
    second_out,
    second_in,
    own_sum,
    local_sem,
    down_sem,
    up_sem,
    w_sem,
    x_send,
    x_recv,
    a_send,
    a_recv,
    t_send,
    t_recv,
    b_send,
    b_recv,
    c_send,
    c_recv,
    r_send,
    r_recv,
    s_send,
    s_recv,
):
    width = weight.shape[2]
    depth = weight.shape[1]
    half = width // 4
    x, t = lax.axis_index("dp"), lax.axis_index("tp")
    z, y, core, chip = t // 8, (t // 2) % 4, t % 2, t // 2

    quarters = wide.shape[0]

    def put_wide(at, value):
        for j in range(quarters):
            wide[j, at, :] = value[:, j * 128 : (j + 1) * 128]

    def get_wide(at):
        return jnp.concatenate([wide[j, at, :] for j in range(quarters)], axis=1)

    def remote(src, dst, send, recv, device):
        return pltpu.make_async_remote_copy(
            src_ref=src,
            dst_ref=dst,
            send_sem=send,
            recv_sem=recv,
            device_id=device,
            device_id_type=MESH,
        )

    barrier = pltpu.get_barrier_semaphore()

    @pl.loop(1, TP)
    def _(i):
        pl.semaphore_signal(barrier, inc=1, device_id=(x, (t + i) % TP), device_id_type=MESH)

    @pl.loop(1, RING)
    def _(i):
        pl.semaphore_signal(barrier, inc=1, device_id=((x + i) % RING, t), device_id_type=MESH)

    pl.semaphore_wait(barrier, TP - 1 + RING - 1)

    def x_copy(peer, slot):
        return remote(
            slabs_in.at[peer], xrecv.at[slot], x_send.at[peer], x_recv.at[slot], (x, 2 * peer + core)
        )

    @pl.loop(1, CHIPS)
    def _(i):
        peer = (chip + i) % CHIPS
        x_copy(peer, chip).start()

    x_own = pltpu.make_async_copy(slabs_in.at[chip], xrecv.at[chip], local_sem.at[0])
    x_own.start()
    w_out = remote(weight_in, weight.at[core], w_sem.at[0], w_sem.at[1], (x, t + 1 - 2 * core))
    w_out.start()
    w_own = pltpu.make_async_copy(weight_in, weight.at[core], local_sem.at[1])
    w_own.start()

    @pl.loop(0, SLOTS)
    def _(i):
        packed[i] = rows_in[index[0, i]]

    def a_copy(peer, slot):
        return remote(
            packed.at[pl.ds(peer * CAP, CAP)],
            gathered.at[pl.ds(slot * CAP, CAP)],
            a_send.at[peer],
            a_recv.at[slot],
            (peer, t),
        )

    @pl.loop(1, RING)
    def _(i):
        a_copy((x + i) % RING, x).start()

    a_own = pltpu.make_async_copy(
        packed.at[pl.ds(x * CAP, CAP)], gathered.at[pl.ds(x * CAP, CAP)], local_sem.at[2]
    )
    a_own.start()
    a_own.wait()

    @pl.loop(1, RING)
    def _(i):
        peer = (x + i) % RING
        a_copy(peer, peer).wait_recv()

    @pl.loop(1, RING)
    def _(i):
        peer = (x + i) % RING
        a_copy(peer, peer).wait_send()

    @pl.loop(0, SLOTS)
    def _(i):
        packed[i] = gathered[index[1, i]]

    def t_copy(peer, slot):
        return remote(
            packed.at[pl.ds(peer * OWN, OWN)],
            owned.at[pl.ds(slot * OWN, OWN)],
            t_send.at[peer],
            t_recv.at[slot],
            (x, peer),
        )

    @pl.loop(1, TP)
    def _(i):
        t_copy((t + i) % TP, t).start()

    t_own = pltpu.make_async_copy(
        packed.at[pl.ds(t * OWN, OWN)], owned.at[pl.ds(t * OWN, OWN)], local_sem.at[2]
    )
    t_own.start()

    w_own.wait()
    w_out.wait()
    x_own.wait()

    @pl.loop(1, CHIPS)
    def _(i):
        peer = (chip + i) % CHIPS
        x_copy(peer, peer).wait_recv()

    def axes(p):
        return (y, z) if p == 0 else (z, y)

    def device(p, a, b):
        return (x, (b * RING + a if p == 0 else a * RING + b) * 2 + core)

    def partial_sum(p, a_to, column):
        b = axes(p)[1]
        total = None
        for k in range(2):
            left = []
            for i in range(RING):
                b_to = (b + i) % RING
                at = b_to * RING + a_to if p == 0 else a_to * RING + b_to
                left.append(xrecv[at, k * HOME : (k + 1) * HOME, :][:, :depth])
            term = jnp.dot(
                jnp.concatenate(left, axis=0),
                weight[k, :, pl.ds(column, TILE)],
                preferred_element_type=F32,
            )
            total = term if total is None else total + term
        return total

    def fill(p, slot, a_to, side, added=None):
        @pl.loop(0, half // TILE)
        def _(n):
            col = pl.multiple_of(n * TILE, TILE)
            total = partial_sum(p, a_to, pl.multiple_of((2 * p + side) * half + n * TILE, TILE))
            if added is not None:
                total = total + relay[p, added, :, pl.ds(col, TILE)].astype(F32)
            parts[p, slot, :, pl.ds(col, TILE)] = total.astype(BF16)

    def r_copy(p, k):
        a, b = axes(p)
        up_to, down_to = device(p, (a + 1) % RING, b), device(p, (a + 3) % RING, b)
        src, dst, to = [
            (0, relay.at[p, 0], up_to),
            (1, relay.at[p, 1], down_to),
            (2, fin_hbm.at[p, 1], up_to),
            (3, fin_hbm.at[p, 2], down_to),
            (0, fin_hbm.at[p, 0], up_to),
            (1, fin_hbm.at[p, 3], down_to),
        ][k]
        return remote(parts.at[p, src], dst, r_send.at[p, k], r_recv.at[p, k], to)

    for p in range(2):
        a, b = axes(p)
        for k in range(2):
            fill(p, k, (a + 2) % RING, k)
            r_copy(p, k).start()
    for p in range(2):
        a, b = axes(p)
        fill(p, 2, (a + 1) % RING, 1)
        r_copy(p, 2).start()
        fill(p, 3, (a + 3) % RING, 0)
        r_copy(p, 3).start()
    for p in range(2):
        a, b = axes(p)
        for k in range(2):
            r_copy(p, k).wait()
            fill(p, k, (a + 1 + 2 * k) % RING, k, added=k)
            r_copy(p, 4 + k).start()

    t_own.wait()

    @pl.loop(1, TP)
    def _(i):
        peer = (t + i) % TP
        t_copy(peer, peer).wait_recv()

    chunks = down_in.shape[1] // LANES

    def down_copy(s):
        return pltpu.make_async_copy(
            down_in.at[:, pl.ds(pl.multiple_of(s * LANES, LANES), LANES)],
            down.at[s % 2],
            down_sem.at[s % 2],
        )

    def up_copy(s):
        return pltpu.make_async_copy(
            up_in.at[:, pl.ds(pl.multiple_of(s * TILE, TILE), TILE)], up.at[s % 2], up_sem.at[s % 2]
        )

    down_copy(0).start()
    up_copy(0).start()
    part = SLOTS // 2
    for k in range(2):

        @pl.loop(0, part)
        def _(i):
            put_wide(pl.ds(i * SLAB_ROWS, SLAB_ROWS), owned[k * part + i].astype(F32))

        @pl.loop(0, chunks + 1)
        def _(s):
            piece = get_wide(pl.ds(s, part, stride=SLAB_ROWS)).astype(BF16)
            for j in range(OWN):
                lo, hi = max(j * SLAB_ROWS, k * part), min((j + 1) * SLAB_ROWS, (k + 1) * part)
                if lo < hi:
                    gathered[s * OWN + j, lo - j * SLAB_ROWS : hi - j * SLAB_ROWS, :] = piece[
                        lo - k * part : hi - k * part
                    ]

    def latent_term(s, factors):
        left = gathered[pl.ds(s * OWN, OWN)].reshape(SLOTS, LANES)
        return lax.dot_general(left, factors, (((1,), (1,)), ((), ())), preferred_element_type=F32)

    def latent_step(s, total):
        @pl.when(s + 1 < chunks)
        def _():
            down_copy(s + 1).start()

        down_copy(s).wait()
        return total + latent_term(s, down[s % 2])

    latent = lax.fori_loop(0, chunks, latent_step, latent_term(chunks, down_tail[...]))
    latent = (latent * gains[...]).astype(BF16)

    @pl.loop(0, OUT_ROWS)
    def _(s):
        @pl.when(s + 1 < OUT_ROWS)
        def _():
            up_copy(s + 1).start()

        up_copy(s).wait()
        put_wide(
            pl.ds(s, SLOTS, stride=OUT_ROWS),
            jnp.dot(latent, up[s % 2], preferred_element_type=F32),
        )

    @pl.loop(0, SLOTS)
    def _(i):
        back_out[i] = get_wide(pl.ds(i * OUT_ROWS, OUT_ROWS)).astype(BF16)

    def b_copy(peer, slot):
        return remote(
            back_out.at[pl.ds(peer * OWN, OWN)],
            back_in.at[pl.ds(slot * OWN, OWN)],
            b_send.at[peer],
            b_recv.at[slot],
            (x, peer),
        )

    @pl.loop(1, TP)
    def _(i):
        b_copy((t + i) % TP, t).start()

    b_own = pltpu.make_async_copy(
        back_out.at[pl.ds(t * OWN, OWN)], back_in.at[pl.ds(t * OWN, OWN)], local_sem.at[2]
    )
    b_own.start()

    def s_copy(p, d):
        a, b = axes(p)
        return remote(
            second_out.at[p, d - 1],
            second_in.at[p, d - 1],
            s_send.at[p, d - 1],
            s_recv.at[p, d - 1],
            device(p, a, (b + d) % RING),
        )

    for p in range(2):
        a, b = axes(p)
        for k in range(2):
            r_copy(p, 2 + k).wait()
            r_copy(p, 4 + k).wait()
        fin = pltpu.make_async_copy(fin_hbm.at[p], parts.at[p], local_sem.at[3])
        fin.start()
        fin.wait()
        for side in range(2):

            @pl.loop(0, half // TILE)
            def _(n):
                col = pl.multiple_of(n * TILE, TILE)
                at = pl.multiple_of(side * half + n * TILE, TILE)
                total = partial_sum(p, a, pl.multiple_of((2 * p + side) * half + n * TILE, TILE))
                total = total + parts[p, side, :, pl.ds(col, TILE)].astype(F32)
                total = total + parts[p, 2 + side, :, pl.ds(col, TILE)].astype(F32)
                own_sum[p, :, pl.ds(at, TILE)] = total[:HOME]
                for d in range(1, RING):
                    second_out[p, d - 1, :, pl.ds(at, TILE)] = total[
                        d * HOME : (d + 1) * HOME
                    ].astype(BF16)

        for d in range(1, RING):
            s_copy(p, d).start()

    b_own.wait()

    @pl.loop(1, TP)
    def _(i):
        peer = (t + i) % TP
        b_copy(peer, peer).wait_recv()

    @pl.loop(0, SLOTS)
    def _(i):
        home_out[i] = back_in[index[2, i]]

    def c_copy(peer, slot):
        return remote(
            home_out.at[pl.ds(peer * CAP, CAP)],
            home_in.at[pl.ds(slot * CAP, CAP)],
            c_send.at[peer],
            c_recv.at[slot],
            (peer, t),
        )

    @pl.loop(1, RING)
    def _(i):
        c_copy((x + i) % RING, x).start()

    c_own = pltpu.make_async_copy(
        home_out.at[pl.ds(x * CAP, CAP)], home_in.at[pl.ds(x * CAP, CAP)], local_sem.at[2]
    )
    c_own.start()

    for p in range(2):
        for d in range(1, RING):
            s_copy(p, d).wait()
    c_own.wait()

    @pl.loop(1, RING)
    def _(i):
        peer = (x + i) % RING
        c_copy(peer, peer).wait_recv()

    @pl.loop(0, HOME)
    def _(i):
        put_wide(pl.ds(i * OUT_ROWS, OUT_ROWS), home_in[index[3, i]].astype(F32))

    for p in range(2):

        @pl.loop(0, OUT_ROWS // 2)
        def _(n):
            at = pl.multiple_of(n * TILE, TILE)
            total = own_sum[p, :, pl.ds(at, TILE)]
            for d in range(3):
                total = total + second_in[p, d, :, pl.ds(at, TILE)].astype(F32)
            total = total + get_wide(pl.ds(p * (OUT_ROWS // 2) + n, HOME, stride=OUT_ROWS))
            out[:, pl.ds(pl.multiple_of(p * 2 * half + n * TILE, TILE), TILE)] = total.astype(BF16)

    @pl.loop(1, CHIPS)
    def _(i):
        peer = (chip + i) % CHIPS
        x_copy(peer, peer).wait_send()

    @pl.loop(1, TP)
    def _(i):
        peer = (t + i) % TP
        t_copy(peer, peer).wait_send()
        b_copy(peer, peer).wait_send()

    @pl.loop(1, RING)
    def _(i):
        peer = (x + i) % RING
        c_copy(peer, peer).wait_send()


def local(
    hidden,
    draft_row_client,
    client_rank_bin,
    client_device,
    down_weight,
    packed_down_factors,
    packed_up_factors,
):
    depth, width = down_weight.shape
    rank_columns = packed_down_factors.shape[1]
    home_index, owner_index, back_index, final_index, start, count, gain = routing(
        draft_row_client, client_rank_bin, client_device
    )
    index = jnp.stack(
        [home_index, owner_index, back_index, jnp.pad(final_index, (0, SLOTS - HOME))]
    ).astype(jnp.int32)
    span = jnp.arange(rank_columns, dtype=jnp.int32)[None, :]
    inside = (span >= start[:, None]) & (span < (start + count)[:, None])
    gains = jnp.where(inside, gain[:, None], 0.0)
    units = hidden.shape[1]
    rows = jnp.pad(hidden, ((0, 0), (0, SLAB_ROWS * LANES - units)))
    rows = rows.reshape(HOME, SLAB_ROWS, LANES)
    slabs = jnp.pad(hidden.reshape(HOME, TP, depth), ((0, 0), (0, 0), (0, LANES - depth)))
    slabs = jnp.transpose(slabs, (1, 0, 2)).reshape(CHIPS, 2 * HOME, LANES)
    down = packed_down_factors.T
    tail = units // LANES * LANES
    down_tail = jnp.pad(down[:, tail:], ((0, 0), (0, LANES - units + tail)))

    vmem, hbm = pl.BlockSpec(memory_space=pltpu.VMEM), pl.BlockSpec(memory_space=pl.ANY)
    dma = pltpu.SemaphoreType.DMA
    half = width // 4
    out, _ = pl.pallas_call(
        body,
        out_shape=(
            jax.ShapeDtypeStruct((HOME, width), BF16),
            jax.ShapeDtypeStruct((2, 4, RING * HOME, half), BF16),
        ),
        in_specs=[pl.BlockSpec(memory_space=pltpu.SMEM), vmem, vmem, hbm, hbm, hbm, vmem, hbm],
        out_specs=(vmem, hbm),
        scratch_shapes=[
            pltpu.VMEM((CHIPS, 2 * HOME, LANES), BF16),
            pltpu.VMEM((2, depth, width), BF16),
            pltpu.VMEM((SLOTS, SLAB_ROWS, LANES), BF16),
            pltpu.VMEM((SLOTS, SLAB_ROWS, LANES), BF16),
            pltpu.VMEM((SLOTS, SLAB_ROWS, LANES), BF16),
            pltpu.VMEM((TILE // 128, SLOTS * OUT_ROWS, 128), F32),
            pltpu.VMEM((2, rank_columns, LANES), BF16),
            pltpu.VMEM((2, rank_columns, TILE), BF16),
            pltpu.VMEM((SLOTS, OUT_ROWS, TILE), BF16),
            pltpu.VMEM((SLOTS, OUT_ROWS, TILE), BF16),
            pltpu.VMEM((SLOTS, OUT_ROWS, TILE), BF16),
            pltpu.VMEM((SLOTS, OUT_ROWS, TILE), BF16),
            pltpu.VMEM((2, 4, RING * HOME, half), BF16),
            pltpu.VMEM((2, 2, RING * HOME, half), BF16),
            pltpu.VMEM((2, 3, HOME, 2 * half), BF16),
            pltpu.VMEM((2, 3, HOME, 2 * half), BF16),
            pltpu.VMEM((2, HOME, 2 * half), F32),
            dma((4,)),
            dma((2,)),
            dma((2,)),
            dma((2,)),
            dma((CHIPS,)),
            dma((CHIPS,)),
            dma((RING,)),
            dma((RING,)),
            dma((TP,)),
            dma((TP,)),
            dma((TP,)),
            dma((TP,)),
            dma((RING,)),
            dma((RING,)),
            dma((2, 6)),
            dma((2, 6)),
            dma((2, 3)),
            dma((2, 3)),
        ],
        compiler_params=pltpu.CompilerParams(
            collective_id=0, has_side_effects=True, vmem_limit_bytes=63 << 20
        ),
        name="verify_rows",
    )(index, gains, rows, slabs, down_weight, down, down_tail, packed_up_factors)
    return out


def solution(mesh):
    placed = (
        P(("dp", "tp"), None),
        P(("dp", "tp")),
        P(),
        P(),
        P("tp", None),
        P(None, ("dp", "tp")),
        P(("dp", "tp"), None),
    )
    return jax.shard_map(
        local, mesh=mesh, in_specs=placed, out_specs=P(("dp", "tp"), None), check_vma=False
    )
```

```python
import functools

import jax
import jax.numpy as jnp
from jax import lax
from jax.experimental import pallas as pl
from jax.experimental.pallas import tpu as pltpu
from jax.sharding import PartitionSpec as P

MESH = pl.DeviceIdType.MESH
BF16 = jnp.bfloat16
F32 = jnp.float32
adapter_scale_fn = 4.0

RING = 4
CHIPS = RING * RING
TP = 2 * CHIPS
HOME = 64
CAP = 24
OWN = 3
SLOTS = RING * CAP
LANES = 512
TILE = 512
SLAB_ROWS = TP
PART = SLAB_ROWS // 2
OUT = 256
AHEAD = 8
UP_AHEAD = 4


def prefix_count(match):
    n = match.shape[0]
    order = jnp.arange(n, dtype=jnp.int32)
    tri = (order[None, :] <= order[:, None]).astype(BF16)
    return jnp.dot(tri, match.astype(BF16), preferred_element_type=F32).astype(jnp.int32)


def lookup(index, table):
    hit = index[:, None] == jnp.arange(table.shape[0], dtype=jnp.int32)[None, :]
    return jnp.sum(jnp.where(hit, table[None, :], 0), axis=1)


def place(target, value, size):
    hit = jnp.arange(size, dtype=jnp.int32)[:, None] == target[None, :]
    return jnp.sum(jnp.where(hit, value[None, :], 0), axis=1)


def routing(draft_row_client, client_rank_bin, client_device, rank_columns):
    x, t = lax.axis_index("dp"), lax.axis_index("tp")
    slots = jnp.arange(SLOTS, dtype=jnp.int32)

    def send(values, axis, parts):
        return lax.all_to_all(
            values.reshape(parts, SLOTS // parts), axis, split_axis=0, concat_axis=0, tiled=True
        ).reshape(SLOTS)

    group = lookup(draft_row_client, client_device) // TP
    hit = group[:, None] == jnp.arange(RING, dtype=jnp.int32)[None, :]
    rank = jnp.sum(jnp.where(hit, prefix_count(hit) - 1, 0), axis=1)
    slot_of_row = group * CAP + rank
    home_index = place(slot_of_row, jnp.arange(HOME, dtype=jnp.int32), SLOTS)

    tenant = send(place(slot_of_row, draft_row_client + 1, SLOTS), "dp", RING) - 1
    position = lookup(tenant, client_device) % TP
    hit = (position[:, None] == jnp.arange(TP, dtype=jnp.int32)[None, :]) & (tenant >= 0)[:, None]
    rank = jnp.sum(jnp.where(hit, prefix_count(hit) - 1, 0), axis=1)
    owner = jnp.where(tenant >= 0, position * OWN + rank, -1)
    owner_index = place(owner, slots, SLOTS)
    back_index = jnp.maximum(owner, 0)

    index = jnp.stack(
        [home_index, owner_index, back_index, jnp.pad(slot_of_row, (0, SLOTS - HOME))]
    )

    tenant_id = jnp.arange(client_device.shape[0], dtype=jnp.int32)
    here = client_device == x * TP + t
    first = jnp.min(jnp.where(here, tenant_id, client_device.shape[0]))
    second = jnp.max(jnp.where(here, tenant_id, -1))
    first_rank = jnp.sum(jnp.where(tenant_id == first, client_rank_bin, 0))
    second_rank = jnp.sum(jnp.where(tenant_id == second, client_rank_bin, 0))
    span = jnp.arange(rank_columns, dtype=jnp.int32)
    after = span >= first_rank
    gains = adapter_scale_fn / jnp.sqrt(jnp.stack([first_rank, second_rank]).astype(F32))
    gains = jnp.stack(
        [
            jnp.where(after, 0.0, gains[0]),
            jnp.where(after & (span < first_rank + second_rank), gains[1], 0.0),
            jnp.full(rank_columns, first + 1, F32),
            jnp.full(rank_columns, second + 1, F32),
        ]
    )
    return index.astype(jnp.int32), jnp.pad(gains, ((0, 4), (0, 0)))


def body(
    index,
    gains,
    marks,
    hidden,
    weight_in,
    down_in,
    down_tail,
    up_in,
    out,
    fin_hbm,
    slabs,
    rows,
    xrecv,
    weight,
    packed,
    group_first,
    group_second,
    owned,
    wide,
    down,
    up,
    home_in,
    parts,
    relay,
    second_out,
    second_in,
    own_sum,
    latents,
    local_sem,
    down_sem,
    up_sem,
    w_sem,
    x_send,
    x_recv,
    a_send,
    a_recv,
    t_send,
    t_recv,
    b_send,
    b_recv,
    c_send,
    c_recv,
    r_send,
    r_recv,
    s_send,
    s_recv,
):
    width = weight.shape[2]
    depth = weight.shape[1]
    half = width // 4
    x, t = lax.axis_index("dp"), lax.axis_index("tp")
    z, y, core, chip = t // 8, (t // 2) % 4, t % 2, t // 2

    def put_wide(at, value):
        for j in range(value.shape[1] // 128):
            wide[j, at, :] = value[:, j * 128 : (j + 1) * 128]

    def get_wide(at, columns=LANES):
        return jnp.concatenate([wide[j, at, :] for j in range(columns // 128)], axis=1)

    def remote(src, dst, send, recv, device):
        return pltpu.make_async_remote_copy(
            src_ref=src,
            dst_ref=dst,
            send_sem=send,
            recv_sem=recv,
            device_id=device,
            device_id_type=MESH,
        )

    barrier = pltpu.get_barrier_semaphore()

    @pl.loop(1, TP)
    def _(i):
        pl.semaphore_signal(barrier, inc=1, device_id=(x, (t + i) % TP), device_id_type=MESH)

    @pl.loop(1, RING)
    def _(i):
        pl.semaphore_signal(barrier, inc=1, device_id=((x + i) % RING, t), device_id_type=MESH)

    for s in range(TP):
        low = s * depth // 128 * 128
        cover = hidden[:, low : low + LANES + 128].astype(F32)
        cover = pltpu.roll(cover, (LANES + 128 + low - s * depth) % (LANES + 128), 1)
        slabs[s // 2, s % 2 * HOME : (s % 2 + 1) * HOME, :] = cover[:, :LANES].astype(BF16)

    pl.semaphore_wait(barrier, TP - 1 + RING - 1)

    def others(count, me, act):
        @pl.loop(1, count)
        def _(i):
            act((me + i) % count)

    def x_copy(peer, slot):
        return remote(
            slabs.at[peer], xrecv.at[slot], x_send.at[peer], x_recv.at[slot], (x, 2 * peer + core)
        )

    x_own = pltpu.make_async_copy(slabs.at[chip], xrecv.at[chip], local_sem.at[0])
    w_out = remote(weight_in, weight.at[core], w_sem.at[0], w_sem.at[1], (x, t + 1 - 2 * core))
    w_own = pltpu.make_async_copy(weight_in, weight.at[core], local_sem.at[1])

    def base_start():
        others(CHIPS, chip, lambda peer: x_copy(peer, chip).start())
        x_own.start()
        w_out.start()
        w_own.start()

    def base_arrived():
        w_own.wait()
        w_out.wait()
        x_own.wait()
        others(CHIPS, chip, lambda peer: x_copy(peer, peer).wait_recv())

    groups = (group_first, group_second)
    chunks = hidden.shape[1] // LANES

    def rows_ready():
        few = HOME // 2
        for k in range(2):
            own = slice(k * few, (k + 1) * few)

            @pl.loop(0, chunks)
            def _(c):
                put_wide(
                    pl.ds(c, few, stride=SLAB_ROWS),
                    hidden[own, pl.ds(pl.multiple_of(c * LANES, LANES), LANES)].astype(F32),
                )

            for c in range(chunks, SLAB_ROWS - 1):
                put_wide(pl.ds(c, few, stride=SLAB_ROWS), jnp.zeros((few, LANES), F32))
            for j in range(LANES // 128):
                wide[j, pl.ds(SLAB_ROWS - 1, few, stride=SLAB_ROWS), :] = marks[own, :]

            @pl.loop(0, few)
            def _(i):
                rows[k * few + i] = get_wide(pl.ds(i * SLAB_ROWS, SLAB_ROWS)).astype(BF16)

    def a_copy(h, peer, slot):
        return remote(
            packed.at[pl.ds(peer * CAP, CAP), pl.ds(h * PART, PART)],
            groups[h].at[pl.ds(slot * CAP, CAP)],
            a_send.at[h, peer],
            a_recv.at[h, slot],
            (peer, t),
        )

    def a_own(h):
        return pltpu.make_async_copy(
            packed.at[pl.ds(x * CAP, CAP), pl.ds(h * PART, PART)],
            groups[h].at[pl.ds(x * CAP, CAP)],
            local_sem.at[4 + h],
        )

    def group_start():
        @pl.loop(0, SLOTS)
        def _(i):
            packed[i] = rows[index[0, i]]

        for h in range(2):
            others(RING, x, lambda peer: a_copy(h, peer, x).start())
            a_own(h).start()

    def t_copy(h, peer, slot):
        return remote(
            packed.at[pl.ds(peer * OWN, OWN), pl.ds(h * PART, PART)],
            owned.at[pl.ds(slot * OWN, OWN), pl.ds(h * PART, PART)],
            t_send.at[h, peer],
            t_recv.at[h, slot],
            (x, peer),
        )

    def t_own(h):
        return pltpu.make_async_copy(
            packed.at[pl.ds(t * OWN, OWN), pl.ds(h * PART, PART)],
            owned.at[pl.ds(t * OWN, OWN), pl.ds(h * PART, PART)],
            local_sem.at[6 + h],
        )

    def owner_start(h):
        a_own(h).wait()
        others(RING, x, lambda peer: a_copy(h, peer, peer).wait_recv())
        others(RING, x, lambda peer: a_copy(h, peer, peer).wait_send())

        @pl.loop(0, SLOTS)
        def _(i):
            packed[i, h * PART : (h + 1) * PART, :] = groups[h][index[1, i]]

        others(TP, t, lambda peer: t_copy(h, peer, t).start())
        t_own(h).start()

    def axes(p):
        return (y, z) if p == 0 else (z, y)

    def device(p, a, b):
        return (x, (b * RING + a if p == 0 else a * RING + b) * 2 + core)

    def partial_sum(p, a_to, column):
        b = axes(p)[1]
        total = None
        for k in range(2):
            left = []
            for i in range(RING):
                b_to = (b + i) % RING
                at = b_to * RING + a_to if p == 0 else a_to * RING + b_to
                left.append(xrecv[at, k * HOME : (k + 1) * HOME, :][:, :depth])
            term = jnp.dot(
                jnp.concatenate(left, axis=0),
                weight[k, :, pl.ds(column, TILE)],
                preferred_element_type=F32,
            )
            total = term if total is None else total + term
        return total

    def fill(p, slot, a_to, side, added=None):
        @pl.loop(0, half // TILE)
        def _(n):
            col = pl.multiple_of(n * TILE, TILE)
            total = partial_sum(p, a_to, pl.multiple_of((2 * p + side) * half + n * TILE, TILE))
            if added is not None:
                total = total + relay[p, added, :, pl.ds(col, TILE)].astype(F32)
            parts[p, slot, :, pl.ds(col, TILE)] = total.astype(BF16)

    def r_copy(p, k):
        a, b = axes(p)
        up_to, down_to = device(p, (a + 1) % RING, b), device(p, (a + 3) % RING, b)
        src, dst, to = [
            (0, relay.at[p, 0], up_to),
            (1, relay.at[p, 1], down_to),
            (2, fin_hbm.at[p, 1], up_to),
            (3, fin_hbm.at[p, 2], down_to),
            (0, fin_hbm.at[p, 0], up_to),
            (1, fin_hbm.at[p, 3], down_to),
        ][k]
        return remote(parts.at[p, src], dst, r_send.at[p, k], r_recv.at[p, k], to)

    def reduce_far(p):
        for k in range(2):
            fill(p, k, (axes(p)[0] + 2) % RING, k)
            r_copy(p, k).start()

    def reduce_near(p):
        for k in range(2):
            fill(p, 2 + k, (axes(p)[0] + 1 + 2 * k) % RING, 1 - k)
            r_copy(p, 2 + k).start()

    def reduce_pass(p):
        for k in range(2):
            r_copy(p, k).wait()
            fill(p, k, (axes(p)[0] + 1 + 2 * k) % RING, k, added=k)
            r_copy(p, 4 + k).start()

    def down_copy(s):
        return pltpu.make_async_copy(
            down_in.at[:, pl.ds(pl.multiple_of(s * LANES, LANES), LANES)],
            down.at[s % AHEAD],
            down_sem.at[s % AHEAD],
        )

    def up_copy(s):
        return pltpu.make_async_copy(
            up_in.at[:, pl.ds(pl.multiple_of(s * TILE, TILE), TILE)],
            up.at[s % UP_AHEAD],
            up_sem.at[s % UP_AHEAD],
        )

    def factors_start():
        for s in range(AHEAD):
            down_copy(s).start()
        for s in range(UP_AHEAD):
            up_copy(s).start()

    def latent_part(h):
        t_own(h).wait()
        others(TP, t, lambda peer: t_copy(h, peer, peer).wait_recv())

        @pl.loop(0, SLOTS)
        def _(i):
            put_wide(
                pl.ds(i * PART, PART), owned[i, h * PART : (h + 1) * PART, :].astype(F32)
            )

        first, last = h * PART, min((h + 1) * PART, chunks)

        @pl.loop(0, last - first)
        def _(s):
            piece = get_wide(pl.ds(s, SLOTS, stride=PART)).astype(BF16)
            rows[pl.ds(s * OWN, OWN)] = piece.reshape(OWN, SLAB_ROWS, LANES)

        def term(s, factors):
            left = rows[pl.ds((s - first) * OWN, OWN)].reshape(SLOTS, LANES)
            return lax.dot_general(
                left, factors, (((1,), (1,)), ((), ())), preferred_element_type=F32
            )

        def step(s, total):
            down_copy(s).wait()
            total = total + term(s, down[s % AHEAD])

            @pl.when(s + AHEAD < chunks - 1)
            def _():
                down_copy(s + AHEAD).start()

            return total

        if h == 0:
            start = jnp.zeros(latents.shape, F32)
        else:
            start = latents[...] + term(chunks - 1, down_tail[...])
        total = lax.fori_loop(first, min(last, chunks - 1), step, start)
        if h == 1:
            mark = get_wide(pl.ds(PART - 1, SLOTS, stride=PART))[:, : latents.shape[1]]
            total = total * (
                jnp.where(mark == gains[2:3, :], gains[0:1, :], 0.0)
                + jnp.where(mark == gains[3:4, :], gains[1:2, :], 0.0)
            )
        latents[...] = total

    def b_copy(h, peer, slot):
        return remote(
            packed.at[pl.ds(peer * OWN, OWN), pl.ds(h * PART, PART), pl.ds(0, OUT)],
            groups[h].at[pl.ds(slot * OWN, OWN), :, pl.ds(0, OUT)],
            b_send.at[h, peer],
            b_recv.at[h, slot],
            (x, peer),
        )

    def b_own(h):
        return pltpu.make_async_copy(
            packed.at[pl.ds(t * OWN, OWN), pl.ds(h * PART, PART), pl.ds(0, OUT)],
            groups[h].at[pl.ds(t * OWN, OWN), :, pl.ds(0, OUT)],
            local_sem.at[8 + h],
        )

    def back_start(h):
        steps = up_in.shape[1] // TILE
        left = latents[...].astype(BF16)
        others(TP, t, lambda peer: t_copy(h, peer, peer).wait_send())

        @pl.loop(h * steps // 2, (h + 1) * steps // 2)
        def _(s):
            up_copy(s).wait()
            product = jnp.dot(left, up[s % UP_AHEAD], preferred_element_type=F32)
            for j in range(TILE // OUT):
                put_wide(
                    pl.ds((s - h * (steps // 2)) * (TILE // OUT) + j, SLOTS, stride=PART),
                    product[:, j * OUT : (j + 1) * OUT],
                )

            @pl.when(s + UP_AHEAD < steps)
            def _():
                up_copy(s + UP_AHEAD).start()

        @pl.loop(0, SLOTS)
        def _(i):
            packed[i, h * PART : (h + 1) * PART, :OUT] = get_wide(
                pl.ds(i * PART, PART), OUT
            ).astype(BF16)

        others(TP, t, lambda peer: b_copy(h, peer, t).start())
        b_own(h).start()

    def s_copy(p, d):
        a, b = axes(p)
        return remote(
            second_out.at[p, d - 1],
            second_in.at[p, d - 1],
            s_send.at[p, d - 1],
            s_recv.at[p, d - 1],
            device(p, a, (b + d) % RING),
        )

    def reduce_second(p):
        for k in range(2, 6):
            r_copy(p, k).wait()
        fin = pltpu.make_async_copy(fin_hbm.at[p], parts.at[p], local_sem.at[2 + p])
        fin.start()
        fin.wait()
        for side in range(2):

            @pl.loop(0, half // TILE)
            def _(n):
                col = pl.multiple_of(n * TILE, TILE)
                at = pl.multiple_of(side * half + n * TILE, TILE)
                total = partial_sum(
                    p, axes(p)[0], pl.multiple_of((2 * p + side) * half + n * TILE, TILE)
                )
                total = total + parts[p, side, :, pl.ds(col, TILE)].astype(F32)
                total = total + parts[p, 2 + side, :, pl.ds(col, TILE)].astype(F32)
                own_sum[p, :, pl.ds(at, TILE)] = total[:HOME]
                for d in range(1, RING):
                    second_out[p, d - 1, :, pl.ds(at, TILE)] = total[
                        d * HOME : (d + 1) * HOME
                    ].astype(BF16)

        for d in range(1, RING):
            s_copy(p, d).start()

    def c_copy(h, peer, slot):
        return remote(
            packed.at[pl.ds(peer * CAP, CAP), pl.ds(h * PART, PART), pl.ds(OUT, OUT)],
            home_in.at[pl.ds(slot * CAP, CAP), pl.ds(h * PART, PART)],
            c_send.at[h, peer],
            c_recv.at[h, slot],
            (peer, t),
        )

    def c_own(h):
        return pltpu.make_async_copy(
            packed.at[pl.ds(x * CAP, CAP), pl.ds(h * PART, PART), pl.ds(OUT, OUT)],
            home_in.at[pl.ds(x * CAP, CAP), pl.ds(h * PART, PART)],
            local_sem.at[10 + h],
        )

    def home_start(h):
        b_own(h).wait()
        others(TP, t, lambda peer: b_copy(h, peer, peer).wait_recv())

        @pl.loop(0, SLOTS)
        def _(i):
            packed[i, h * PART : (h + 1) * PART, OUT:] = groups[h][index[2, i]][:, :OUT]

        others(RING, x, lambda peer: c_copy(h, peer, x).start())
        c_own(h).start()

    def second_arrived():
        for p in range(2):
            for d in range(1, RING):
                s_copy(p, d).wait()

    def home_arrived(h):
        c_own(h).wait()
        others(RING, x, lambda peer: c_copy(h, peer, peer).wait_recv())

    def finish():
        few = HOME // 2
        for k in range(2):
            own = slice(k * few, (k + 1) * few)

            @pl.loop(0, few)
            def _(i):
                put_wide(pl.ds(i * SLAB_ROWS, SLAB_ROWS), home_in[index[3, k * few + i]].astype(F32))

            for p in range(2):

                @pl.loop(0, PART)
                def _(n):
                    at = pl.ds(pl.multiple_of(n * OUT, OUT), OUT)
                    total = own_sum[p, own, at]
                    for d in range(3):
                        total = total + second_in[p, d, own, at].astype(F32)
                    total = total + get_wide(pl.ds(p * PART + n, few, stride=SLAB_ROWS), OUT)
                    column = pl.multiple_of(p * 2 * half + n * OUT, OUT)
                    out[own, pl.ds(column, OUT)] = total.astype(BF16)

    def all_left():
        others(CHIPS, chip, lambda peer: x_copy(peer, peer).wait_send())
        for h in range(2):
            others(TP, t, lambda peer: b_copy(h, peer, peer).wait_send())
            others(RING, x, lambda peer: c_copy(h, peer, peer).wait_send())

    base_start()
    factors_start()
    rows_ready()
    group_start()
    owner_start(0)
    base_arrived()
    reduce_far(0)
    owner_start(1)
    reduce_far(1)
    reduce_near(0)
    reduce_near(1)
    latent_part(0)
    reduce_pass(0)
    reduce_pass(1)
    latent_part(1)
    back_start(0)
    back_start(1)
    reduce_second(0)
    home_start(0)
    reduce_second(1)
    home_start(1)
    second_arrived()
    home_arrived(0)
    home_arrived(1)
    finish()
    all_left()


def local(
    hidden,
    draft_row_client,
    client_rank_bin,
    client_device,
    down_weight,
    packed_down_factors,
    packed_up_factors,
):
    depth, width = down_weight.shape
    rank_columns = packed_down_factors.shape[1]
    index, gains = routing(draft_row_client, client_rank_bin, client_device, rank_columns)
    units = hidden.shape[1]
    padded = -(-units // LANES) * LANES
    marks = jnp.broadcast_to((draft_row_client + 1).astype(F32)[:, None], (HOME, 128))
    rows = jnp.pad(hidden, ((0, 0), (0, padded - units)))
    down = packed_down_factors.T
    tail = units // LANES * LANES
    down_tail = jnp.pad(down[:, tail:], ((0, 0), (0, LANES - units + tail)))

    vmem, hbm = pl.BlockSpec(memory_space=pltpu.VMEM), pl.BlockSpec(memory_space=pl.ANY)
    dma = pltpu.SemaphoreType.DMA
    half = width // 4
    out, _ = pl.pallas_call(
        body,
        out_shape=(
            jax.ShapeDtypeStruct((HOME, width), BF16),
            jax.ShapeDtypeStruct((2, 4, RING * HOME, half), BF16),
        ),
        in_specs=[pl.BlockSpec(memory_space=pltpu.SMEM), vmem, vmem, vmem, hbm, hbm, vmem, hbm],
        out_specs=(vmem, hbm),
        scratch_shapes=[
            pltpu.VMEM((CHIPS, 2 * HOME, LANES), BF16),
            pltpu.VMEM((HOME, SLAB_ROWS, LANES), BF16),
            pltpu.VMEM((CHIPS, 2 * HOME, LANES), BF16),
            pltpu.VMEM((2, depth, width), BF16),
            pltpu.VMEM((SLOTS, SLAB_ROWS, LANES), BF16),
            pltpu.VMEM((SLOTS, PART, LANES), BF16),
            pltpu.VMEM((SLOTS, PART, LANES), BF16),
            pltpu.VMEM((SLOTS, SLAB_ROWS, LANES), BF16),
            pltpu.VMEM((LANES // 128, SLOTS * PART, 128), F32),
            pltpu.VMEM((AHEAD, rank_columns, LANES), BF16),
            pltpu.VMEM((UP_AHEAD, rank_columns, TILE), BF16),
            pltpu.VMEM((SLOTS, SLAB_ROWS, OUT), BF16),
            pltpu.VMEM((2, 4, RING * HOME, half), BF16),
            pltpu.VMEM((2, 2, RING * HOME, half), BF16),
            pltpu.VMEM((2, 3, HOME, 2 * half), BF16),
            pltpu.VMEM((2, 3, HOME, 2 * half), BF16),
            pltpu.VMEM((2, HOME, 2 * half), F32),
            pltpu.VMEM((SLOTS, rank_columns), F32),
            dma((12,)),
            dma((AHEAD,)),
            dma((UP_AHEAD,)),
            dma((2,)),
            dma((CHIPS,)),
            dma((CHIPS,)),
            dma((2, RING)),
            dma((2, RING)),
            dma((2, TP)),
            dma((2, TP)),
            dma((2, TP)),
            dma((2, TP)),
            dma((2, RING)),
            dma((2, RING)),
            dma((2, 6)),
            dma((2, 6)),
            dma((2, 3)),
            dma((2, 3)),
        ],
        compiler_params=pltpu.CompilerParams(
            collective_id=0, has_side_effects=True, vmem_limit_bytes=63 << 20
        ),
        name="verify_rows",
    )(index, gains, marks, rows, down_weight, down, down_tail, packed_up_factors)
    return out


def solution(mesh):
    placed = (
        P(("dp", "tp"), None),
        P(("dp", "tp")),
        P(),
        P(),
        P("tp", None),
        P(None, ("dp", "tp")),
        P(("dp", "tp"), None),
    )
    return jax.shard_map(
        local, mesh=mesh, in_specs=placed, out_specs=P(("dp", "tp"), None), check_vma=False
    )
```

```python
import functools

import jax
import jax.numpy as jnp
from jax import lax
from jax.experimental import pallas as pl
from jax.experimental.pallas import tpu as pltpu
from jax.sharding import PartitionSpec as P

MESH = pl.DeviceIdType.MESH
BF16 = jnp.bfloat16
F32 = jnp.float32
adapter_scale_fn = 4.0

RING = 4
CHIPS = RING * RING
TP = 2 * CHIPS
HOME = 64
CAP = 24
OWN = 3
SLOTS = RING * CAP
LANES = 512
TILE = 512
SLAB_ROWS = TP
PART = SLAB_ROWS // 2
OUT = 256
AHEAD = 8
UP_AHEAD = 4


def tables(client_rank_bin, client_device, rank_columns):
    x, t = lax.axis_index("dp"), lax.axis_index("tp")
    column = jnp.arange(128, dtype=jnp.int32)[None, :]
    device = client_device[:, None]
    places = ((column < TP) & (device == x * TP + column)) | (column == TP + device // TP)

    tenant_id = jnp.arange(client_device.shape[0], dtype=jnp.int32)
    here = client_device == x * TP + t
    first = jnp.min(jnp.where(here, tenant_id, client_device.shape[0]))
    second = jnp.max(jnp.where(here, tenant_id, -1))
    first_rank = jnp.sum(jnp.where(tenant_id == first, client_rank_bin, 0))
    second_rank = jnp.sum(jnp.where(tenant_id == second, client_rank_bin, 0))
    span = jnp.arange(rank_columns, dtype=jnp.int32)[None, :]
    kind = jnp.arange(8, dtype=jnp.int32)[:, None]
    after = span >= first_rank
    gain = adapter_scale_fn / jnp.sqrt(
        jnp.where(kind == 0, first_rank, second_rank).astype(F32)
    )
    inside = jnp.where(kind == 0, ~after, after & (span < first_rank + second_rank))
    marks = jnp.where(kind == 2, first + 1, second + 1).astype(F32)
    gains = jnp.where(kind < 2, jnp.where(inside, gain, 0.0), marks)
    return places.astype(BF16), gains


def body(
    places,
    gains,
    marks,
    hidden,
    weight_in,
    down_in,
    down_tail,
    up_in,
    out,
    fin_hbm,
    slabs,
    rows,
    xrecv,
    weight,
    packed,
    group_first,
    group_second,
    owned,
    wide,
    down,
    up,
    home_in,
    parts,
    relay,
    second_out,
    second_in,
    own_sum,
    latents,
    gain,
    found,
    index,
    local_sem,
    down_sem,
    up_sem,
    w_sem,
    x_send,
    x_recv,
    a_send,
    a_recv,
    t_send,
    t_recv,
    b_send,
    b_recv,
    c_send,
    c_recv,
    r_send,
    r_recv,
    s_send,
    s_recv,
):
    width = weight.shape[2]
    depth = weight.shape[1]
    half = width // 4
    x, t = lax.axis_index("dp"), lax.axis_index("tp")
    z, y, core, chip = t // 8, (t // 2) % 4, t % 2, t // 2

    def put_wide(at, value):
        for j in range(value.shape[1] // 128):
            wide[j, at, :] = value[:, j * 128 : (j + 1) * 128]

    def get_wide(at, columns=LANES):
        return jnp.concatenate([wide[j, at, :] for j in range(columns // 128)], axis=1)

    def remote(src, dst, send, recv, device):
        return pltpu.make_async_remote_copy(
            src_ref=src,
            dst_ref=dst,
            send_sem=send,
            recv_sem=recv,
            device_id=device,
            device_id_type=MESH,
        )

    barrier = pltpu.get_barrier_semaphore()

    @pl.loop(1, TP)
    def _(i):
        pl.semaphore_signal(barrier, inc=1, device_id=(x, (t + i) % TP), device_id_type=MESH)

    @pl.loop(1, RING)
    def _(i):
        pl.semaphore_signal(barrier, inc=1, device_id=((x + i) % RING, t), device_id_type=MESH)

    for s in range(TP):
        low = s * depth // 128 * 128
        cover = hidden[:, low : low + LANES + 128].astype(F32)
        cover = pltpu.roll(cover, (LANES + 128 + low - s * depth) % (LANES + 128), 1)
        slabs[s // 2, s % 2 * HOME : (s % 2 + 1) * HOME, :] = cover[:, :LANES].astype(BF16)

    pl.semaphore_wait(barrier, TP - 1 + RING - 1)

    def others(count, me, act):
        @pl.loop(1, count)
        def _(i):
            act((me + i) % count)

    def x_copy(peer, slot):
        return remote(
            slabs.at[peer], xrecv.at[slot], x_send.at[peer], x_recv.at[slot], (x, 2 * peer + core)
        )

    x_own = pltpu.make_async_copy(slabs.at[chip], xrecv.at[chip], local_sem.at[0])
    w_out = remote(weight_in, weight.at[core], w_sem.at[0], w_sem.at[1], (x, t + 1 - 2 * core))
    w_own = pltpu.make_async_copy(weight_in, weight.at[core], local_sem.at[1])

    def base_start():
        others(CHIPS, chip, lambda peer: x_copy(peer, chip).start())
        x_own.start()
        w_out.start()
        w_own.start()

    def base_arrived():
        w_own.wait()
        w_out.wait()
        x_own.wait()
        others(CHIPS, chip, lambda peer: x_copy(peer, peer).wait_recv())

    def running(hit):
        n = hit.shape[0]
        order = lax.broadcasted_iota(jnp.int32, (n, n), 0) >= lax.broadcasted_iota(
            jnp.int32, (n, n), 1
        )
        return jnp.dot(
            order.astype(F32).astype(BF16), hit.astype(BF16), preferred_element_type=F32
        )

    def target(mark, low, count, capacity):
        n = mark.shape[0]
        column = lax.broadcasted_iota(jnp.int32, (n, 128), 1)
        tenants = [(mark == (column + 1 + k).astype(F32)).astype(F32) for k in (0, 128)]
        hit = jnp.dot(
            jnp.concatenate(tenants, axis=1).astype(BF16), places[...], preferred_element_type=F32
        )
        hit = jnp.where((column >= low) & (column < low + count), hit, 0.0)
        slot = (column - low).astype(F32) * capacity + running(hit) - 1.0
        slot = jnp.sum(hit * slot, axis=1, keepdims=True)
        return jnp.where(jnp.sum(hit, axis=1, keepdims=True) > 0, slot, -1.0)

    def set_index(row, slot, empty):
        n = slot.shape[0]
        column = lax.broadcasted_iota(jnp.int32, (n, 128), 1)
        source = lax.broadcasted_iota(jnp.int32, (n, 128), 0)
        back = jnp.where(slot == column.astype(F32), (source - empty).astype(F32), 0.0)
        forth = jnp.where(source == column, jnp.maximum(slot, 0.0), 0.0)
        found[row] = jnp.broadcast_to(
            jnp.sum(back, axis=0, keepdims=True).astype(jnp.int32) + empty, (8, 128)
        )
        found[row + 1] = jnp.broadcast_to(
            jnp.sum(forth, axis=0, keepdims=True).astype(jnp.int32), (8, 128)
        )
        copy = pltpu.make_async_copy(
            found.at[pl.ds(row, 2)], index.at[pl.ds(row, 2)], local_sem.at[12 + row // 2]
        )
        copy.start()
        copy.wait()

    def at_index(row, i, size):
        return jnp.minimum(jnp.maximum(index[row, 0, i], 0), size - 1)

    groups = (group_first, group_second)
    chunks = hidden.shape[1] // LANES

    def rows_ready():
        few = HOME // 2
        for k in range(2):
            own = slice(k * few, (k + 1) * few)

            for c in range(chunks):
                put_wide(
                    pl.ds(c + c // (PART - 1), few, stride=SLAB_ROWS),
                    hidden[own, c * LANES : (c + 1) * LANES].astype(F32),
                )
            for c in range(chunks + 1, SLAB_ROWS):
                put_wide(pl.ds(c, few, stride=SLAB_ROWS), jnp.zeros((few, LANES), F32))
            for j in range(LANES // 128):
                wide[j, pl.ds(PART - 1, few, stride=SLAB_ROWS), :] = marks[own, :]

            @pl.loop(0, few)
            def _(i):
                rows[k * few + i] = get_wide(pl.ds(i * SLAB_ROWS, SLAB_ROWS)).astype(BF16)

        rows[HOME] = jnp.zeros(rows.shape[1:], BF16)

    def a_copy(h, peer, slot):
        return remote(
            packed.at[pl.ds(peer * CAP, CAP), pl.ds(h * PART, PART)],
            groups[h].at[pl.ds(slot * CAP, CAP)],
            a_send.at[h, peer],
            a_recv.at[h, slot],
            (peer, t),
        )

    def a_own(h):
        return pltpu.make_async_copy(
            packed.at[pl.ds(x * CAP, CAP), pl.ds(h * PART, PART)],
            groups[h].at[pl.ds(x * CAP, CAP)],
            local_sem.at[4 + h],
        )

    def group_start():
        set_index(0, target(marks[...], TP, RING, CAP), HOME)

        @pl.loop(0, SLOTS)
        def _(i):
            packed[i] = rows[at_index(0, i, HOME + 1)]

        for h in range(2):
            others(RING, x, lambda peer: a_copy(h, peer, x).start())
            a_own(h).start()

    def t_copy(h, peer, slot):
        return remote(
            packed.at[pl.ds(peer * OWN, OWN), pl.ds(h * PART, PART)],
            owned.at[pl.ds(slot * OWN, OWN), pl.ds(h * PART, PART)],
            t_send.at[h, peer],
            t_recv.at[h, slot],
            (x, peer),
        )

    def t_own(h):
        return pltpu.make_async_copy(
            packed.at[pl.ds(t * OWN, OWN), pl.ds(h * PART, PART)],
            owned.at[pl.ds(t * OWN, OWN), pl.ds(h * PART, PART)],
            local_sem.at[6 + h],
        )

    def owner_start(h):
        a_own(h).wait()
        others(RING, x, lambda peer: a_copy(h, peer, peer).wait_recv())
        others(RING, x, lambda peer: a_copy(h, peer, peer).wait_send())

        if h == 0:

            @pl.loop(0, SLOTS)
            def _(i):
                wide[0, pl.ds(i * PART, PART), :] = groups[h][i, :, :128].astype(F32)

            mark = wide[0, pl.ds(PART - 1, SLOTS, stride=PART), :]
            set_index(2, target(mark, 0, TP, OWN), 0)

        @pl.loop(0, SLOTS)
        def _(i):
            packed[i, h * PART : (h + 1) * PART, :] = groups[h][at_index(2, i, SLOTS)]

        others(TP, t, lambda peer: t_copy(h, peer, t).start())
        t_own(h).start()

    def axes(p):
        return (y, z) if p == 0 else (z, y)

    def device(p, a, b):
        return (x, (b * RING + a if p == 0 else a * RING + b) * 2 + core)

    def partial_sum(p, a_to, column):
        b = axes(p)[1]
        total = None
        for k in range(2):
            left = []
            for i in range(RING):
                b_to = (b + i) % RING
                at = b_to * RING + a_to if p == 0 else a_to * RING + b_to
                left.append(xrecv[at, k * HOME : (k + 1) * HOME, :][:, :depth])
            term = jnp.dot(
                jnp.concatenate(left, axis=0),
                weight[k, :, pl.ds(column, TILE)],
                preferred_element_type=F32,
            )
            total = term if total is None else total + term
        return total

    def fill(p, slot, a_to, side, added=None):
        @pl.loop(0, half // TILE)
        def _(n):
            col = pl.multiple_of(n * TILE, TILE)
            total = partial_sum(p, a_to, pl.multiple_of((2 * p + side) * half + n * TILE, TILE))
            if added is not None:
                total = total + relay[p, added, :, pl.ds(col, TILE)].astype(F32)
            parts[p, slot, :, pl.ds(col, TILE)] = total.astype(BF16)

    def r_copy(p, k):
        a, b = axes(p)
        up_to, down_to = device(p, (a + 1) % RING, b), device(p, (a + 3) % RING, b)
        src, dst, to = [
            (0, relay.at[p, 0], up_to),
            (1, relay.at[p, 1], down_to),
            (2, fin_hbm.at[p, 1], up_to),
            (3, fin_hbm.at[p, 2], down_to),
            (0, fin_hbm.at[p, 0], up_to),
            (1, fin_hbm.at[p, 3], down_to),
        ][k]
        return remote(parts.at[p, src], dst, r_send.at[p, k], r_recv.at[p, k], to)

    def reduce_far(p):
        for k in range(2):
            fill(p, k, (axes(p)[0] + 2) % RING, k)
            r_copy(p, k).start()

    def reduce_near(p):
        for k in range(2):
            fill(p, 2 + k, (axes(p)[0] + 1 + 2 * k) % RING, 1 - k)
            r_copy(p, 2 + k).start()

    def reduce_pass(p):
        for k in range(2):
            r_copy(p, k).wait()
            fill(p, k, (axes(p)[0] + 1 + 2 * k) % RING, k, added=k)
            r_copy(p, 4 + k).start()

    def down_copy(s):
        return pltpu.make_async_copy(
            down_in.at[:, pl.ds(pl.multiple_of(s * LANES, LANES), LANES)],
            down.at[s % AHEAD],
            down_sem.at[s % AHEAD],
        )

    def up_copy(s):
        return pltpu.make_async_copy(
            up_in.at[:, pl.ds(pl.multiple_of(s * TILE, TILE), TILE)],
            up.at[s % UP_AHEAD],
            up_sem.at[s % UP_AHEAD],
        )

    def factors_start():
        for s in range(AHEAD):
            down_copy(s).start()
        for s in range(UP_AHEAD):
            up_copy(s).start()

    def latent_part(h):
        t_own(h).wait()
        others(TP, t, lambda peer: t_copy(h, peer, peer).wait_recv())

        @pl.loop(0, SLOTS)
        def _(i):
            put_wide(
                pl.ds(i * PART, PART), owned[i, h * PART : (h + 1) * PART, :].astype(F32)
            )

        first, last = h * (PART - 1), PART - 1 if h == 0 else chunks

        @pl.loop(0, last - first)
        def _(s):
            piece = get_wide(pl.ds(s, SLOTS, stride=PART)).astype(BF16)
            rows[pl.ds(s * OWN, OWN)] = piece.reshape(OWN, SLAB_ROWS, LANES)

        def term(s, factors):
            left = rows[pl.ds((s - first) * OWN, OWN)].reshape(SLOTS, LANES)
            return lax.dot_general(
                left, factors, (((1,), (1,)), ((), ())), preferred_element_type=F32
            )

        def step(s, total):
            down_copy(s).wait()
            total = total + term(s, down[s % AHEAD])

            @pl.when(s + AHEAD < chunks - 1)
            def _():
                down_copy(s + AHEAD).start()

            return total

        if h == 0:
            mark = get_wide(pl.ds(PART - 1, SLOTS, stride=PART))[:, : latents.shape[1]]
            gain[...] = jnp.where(mark == gains[2:3, :], gains[0:1, :], 0.0) + jnp.where(
                mark == gains[3:4, :], gains[1:2, :], 0.0
            )

        if h == 0:
            start = jnp.zeros(latents.shape, F32)
        else:
            start = latents[...] + term(chunks - 1, down_tail[...])
        total = lax.fori_loop(first, min(last, chunks - 1), step, start)
        latents[...] = total if h == 0 else total * gain[...]

    def b_copy(h, peer, slot):
        return remote(
            packed.at[pl.ds(peer * OWN, OWN), pl.ds(h * PART, PART), pl.ds(0, OUT)],
            groups[h].at[pl.ds(slot * OWN, OWN), :, pl.ds(0, OUT)],
            b_send.at[h, peer],
            b_recv.at[h, slot],
            (x, peer),
        )

    def b_own(h):
        return pltpu.make_async_copy(
            packed.at[pl.ds(t * OWN, OWN), pl.ds(h * PART, PART), pl.ds(0, OUT)],
            groups[h].at[pl.ds(t * OWN, OWN), :, pl.ds(0, OUT)],
            local_sem.at[8 + h],
        )

    def back_start(h):
        steps = up_in.shape[1] // TILE
        left = latents[...].astype(BF16)
        others(TP, t, lambda peer: t_copy(h, peer, peer).wait_send())

        @pl.loop(h * steps // 2, (h + 1) * steps // 2)
        def _(s):
            up_copy(s).wait()
            product = jnp.dot(left, up[s % UP_AHEAD], preferred_element_type=F32)
            for j in range(TILE // OUT):
                put_wide(
                    pl.ds((s - h * (steps // 2)) * (TILE // OUT) + j, SLOTS, stride=PART),
                    product[:, j * OUT : (j + 1) * OUT],
                )

            @pl.when(s + UP_AHEAD < steps)
            def _():
                up_copy(s + UP_AHEAD).start()

        @pl.loop(0, SLOTS)
        def _(i):
            packed[i, h * PART : (h + 1) * PART, :OUT] = get_wide(
                pl.ds(i * PART, PART), OUT
            ).astype(BF16)

        others(TP, t, lambda peer: b_copy(h, peer, t).start())
        b_own(h).start()

    def s_copy(p, side, d):
        a, b = axes(p)
        return remote(
            second_out.at[p, side, d - 1],
            second_in.at[p, side, d - 1],
            s_send.at[p, side, d - 1],
            s_recv.at[p, side, d - 1],
            device(p, a, (b + d) % RING),
        )

    def reduce_second(p, side):
        came = (4, 3) if side == 0 else (2, 5)
        stage = []
        for i, k in enumerate(came):
            r_copy(p, k).wait_recv()
            slot = side + 2 * i
            stage.append(
                pltpu.make_async_copy(
                    fin_hbm.at[p, slot], parts.at[p, slot], local_sem.at[16 + 4 * p + slot]
                )
            )
        for k in (4 + side, 2 + side):
            r_copy(p, k).wait_send()
        for copy in stage:
            copy.start()
        for copy in stage:
            copy.wait()

        @pl.loop(0, half // TILE)
        def _(n):
            col = pl.multiple_of(n * TILE, TILE)
            at = pl.multiple_of(side * half + n * TILE, TILE)
            total = partial_sum(
                p, axes(p)[0], pl.multiple_of((2 * p + side) * half + n * TILE, TILE)
            )
            total = total + parts[p, side, :, pl.ds(col, TILE)].astype(F32)
            total = total + parts[p, 2 + side, :, pl.ds(col, TILE)].astype(F32)
            own_sum[p, :, pl.ds(at, TILE)] = total[:HOME]
            for d in range(1, RING):
                second_out[p, side, d - 1, :, pl.ds(col, TILE)] = total[
                    d * HOME : (d + 1) * HOME
                ].astype(BF16)

        for d in range(1, RING):
            s_copy(p, side, d).start()

    def c_copy(h, peer, slot):
        return remote(
            packed.at[pl.ds(peer * CAP, CAP), pl.ds(h * PART, PART), pl.ds(OUT, OUT)],
            home_in.at[pl.ds(slot * CAP, CAP), pl.ds(h * PART, PART)],
            c_send.at[h, peer],
            c_recv.at[h, slot],
            (peer, t),
        )

    def c_own(h):
        return pltpu.make_async_copy(
            packed.at[pl.ds(x * CAP, CAP), pl.ds(h * PART, PART), pl.ds(OUT, OUT)],
            home_in.at[pl.ds(x * CAP, CAP), pl.ds(h * PART, PART)],
            local_sem.at[10 + h],
        )

    def home_start(h):
        b_own(h).wait()
        others(TP, t, lambda peer: b_copy(h, peer, peer).wait_recv())

        @pl.loop(0, SLOTS)
        def _(i):
            packed[i, h * PART : (h + 1) * PART, OUT:] = groups[h][at_index(3, i, SLOTS)][:, :OUT]

        others(RING, x, lambda peer: c_copy(h, peer, x).start())
        c_own(h).start()

    def second_arrived():
        for p in range(2):
            for side in range(2):
                for d in range(1, RING):
                    s_copy(p, side, d).wait()

    def home_arrived(h):
        c_own(h).wait()
        others(RING, x, lambda peer: c_copy(h, peer, peer).wait_recv())

    def finish():
        few = HOME // 2
        for k in range(2):
            own = slice(k * few, (k + 1) * few)

            @pl.loop(0, few)
            def _(i):
                put_wide(pl.ds(i * SLAB_ROWS, SLAB_ROWS), home_in[at_index(1, k * few + i, SLOTS)].astype(F32))

            for p in range(2):
                for side in range(2):

                    @pl.loop(0, PART // 2)
                    def _(n):
                        at = pl.ds(pl.multiple_of(n * OUT, OUT), OUT)
                        column = pl.multiple_of(side * half + n * OUT, OUT)
                        total = own_sum[p, own, pl.ds(column, OUT)]
                        for d in range(3):
                            total = total + second_in[p, side, d, own, at].astype(F32)
                        place = p * PART + side * (PART // 2) + n
                        total = total + get_wide(pl.ds(place, few, stride=SLAB_ROWS), OUT)
                        column = pl.multiple_of((2 * p + side) * half + n * OUT, OUT)
                        out[own, pl.ds(column, OUT)] = total.astype(BF16)

    def all_left():
        others(CHIPS, chip, lambda peer: x_copy(peer, peer).wait_send())
        for h in range(2):
            others(TP, t, lambda peer: b_copy(h, peer, peer).wait_send())
            others(RING, x, lambda peer: c_copy(h, peer, peer).wait_send())

    base_start()
    factors_start()
    rows_ready()
    group_start()
    owner_start(0)
    base_arrived()
    reduce_far(0)
    owner_start(1)
    reduce_far(1)
    reduce_near(0)
    reduce_near(1)
    latent_part(0)
    reduce_pass(0)
    reduce_pass(1)
    latent_part(1)
    back_start(0)
    back_start(1)
    reduce_second(0, 0)
    reduce_second(1, 0)
    home_start(0)
    reduce_second(0, 1)
    reduce_second(1, 1)
    home_start(1)
    second_arrived()
    home_arrived(0)
    home_arrived(1)
    finish()
    all_left()


def local(
    hidden,
    draft_row_client,
    client_rank_bin,
    client_device,
    down_weight,
    packed_down_factors,
    packed_up_factors,
):
    depth, width = down_weight.shape
    rank_columns = packed_down_factors.shape[1]
    places, gains = tables(client_rank_bin, client_device, rank_columns)
    units = hidden.shape[1]
    padded = -(-units // LANES) * LANES
    marks = jnp.broadcast_to((draft_row_client + 1).astype(F32)[:, None], (HOME, 128))
    rows = jnp.pad(hidden, ((0, 0), (0, padded - units)))
    down = packed_down_factors.T
    tail = units // LANES * LANES
    down_tail = jnp.pad(down[:, tail:], ((0, 0), (0, LANES - units + tail)))

    vmem, hbm = pl.BlockSpec(memory_space=pltpu.VMEM), pl.BlockSpec(memory_space=pl.ANY)
    dma = pltpu.SemaphoreType.DMA
    half = width // 4
    out, _ = pl.pallas_call(
        body,
        out_shape=(
            jax.ShapeDtypeStruct((HOME, width), BF16),
            jax.ShapeDtypeStruct((2, 4, RING * HOME, half), BF16),
        ),
        in_specs=[vmem, vmem, vmem, vmem, hbm, hbm, vmem, hbm],
        out_specs=(vmem, hbm),
        scratch_shapes=[
            pltpu.VMEM((CHIPS, 2 * HOME, LANES), BF16),
            pltpu.VMEM((HOME + 1, SLAB_ROWS, LANES), BF16),
            pltpu.VMEM((CHIPS, 2 * HOME, LANES), BF16),
            pltpu.VMEM((2, depth, width), BF16),
            pltpu.VMEM((SLOTS, SLAB_ROWS, LANES), BF16),
            pltpu.VMEM((SLOTS, PART, LANES), BF16),
            pltpu.VMEM((SLOTS, PART, LANES), BF16),
            pltpu.VMEM((SLOTS, SLAB_ROWS, LANES), BF16),
            pltpu.VMEM((LANES // 128, SLOTS * PART, 128), F32),
            pltpu.VMEM((AHEAD, rank_columns, LANES), BF16),
            pltpu.VMEM((UP_AHEAD, rank_columns, TILE), BF16),
            pltpu.VMEM((SLOTS, SLAB_ROWS, OUT), BF16),
            pltpu.VMEM((2, 4, RING * HOME, half), BF16),
            pltpu.VMEM((2, 2, RING * HOME, half), BF16),
            pltpu.VMEM((2, 2, 3, HOME, half), BF16),
            pltpu.VMEM((2, 2, 3, HOME, half), BF16),
            pltpu.VMEM((2, HOME, 2 * half), F32),
            pltpu.VMEM((SLOTS, rank_columns), F32),
            pltpu.VMEM((SLOTS, rank_columns), F32),
            pltpu.VMEM((4, 8, 128), jnp.int32),
            pltpu.SMEM((4, 8, 128), jnp.int32),
            dma((24,)),
            dma((AHEAD,)),
            dma((UP_AHEAD,)),
            dma((2,)),
            dma((CHIPS,)),
            dma((CHIPS,)),
            dma((2, RING)),
            dma((2, RING)),
            dma((2, TP)),
            dma((2, TP)),
            dma((2, TP)),
            dma((2, TP)),
            dma((2, RING)),
            dma((2, RING)),
            dma((2, 6)),
            dma((2, 6)),
            dma((2, 2, 3)),
            dma((2, 2, 3)),
        ],
        compiler_params=pltpu.CompilerParams(
            collective_id=0, has_side_effects=True, vmem_limit_bytes=63 << 20
        ),
        name="verify_rows",
    )(places, gains, marks, rows, down_weight, down, down_tail, packed_up_factors)
    return out


def solution(mesh):
    placed = (
        P(("dp", "tp"), None),
        P(("dp", "tp")),
        P(),
        P(),
        P("tp", None),
        P(None, ("dp", "tp")),
        P(("dp", "tp"), None),
    )
    return jax.shard_map(
        local, mesh=mesh, in_specs=placed, out_specs=P(("dp", "tp"), None), check_vma=False
    )
```

```python
import functools

import jax
import jax.numpy as jnp
from jax import lax
from jax.experimental import pallas as pl
from jax.experimental.pallas import tpu as pltpu
from jax.sharding import PartitionSpec as P

MESH = pl.DeviceIdType.MESH
BF16 = jnp.bfloat16
F32 = jnp.float32
adapter_scale_fn = 4.0

RING = 4
CHIPS = RING * RING
TP = 2 * CHIPS
HOME = 64
CAP = 24
OWN = 3
SLOTS = RING * CAP
LANES = 512
TILE = 512
SLAB_ROWS = TP
PART = SLAB_ROWS // 2
OUT = 256
AHEAD = 8
UP_AHEAD = 4


def body(
    tenants,
    rank_bins,
    devices,
    hidden,
    weight_in,
    down_in,
    up_in,
    out,
    fin_hbm,
    slabs,
    rows,
    xrecv,
    weight,
    packed,
    group_first,
    group_second,
    owned,
    wide,
    down,
    down_tail,
    up,
    home_in,
    parts,
    relay,
    second_out,
    second_in,
    own_sum,
    latents,
    gain,
    places,
    gains,
    found,
    index,
    local_sem,
    down_sem,
    up_sem,
    w_sem,
    x_send,
    x_recv,
    a_send,
    a_recv,
    t_send,
    t_recv,
    b_send,
    b_recv,
    c_send,
    c_recv,
    r_send,
    r_recv,
    s_send,
    s_recv,
):
    width = weight.shape[2]
    depth = weight.shape[1]
    half = width // 4
    x, t = lax.axis_index("dp"), lax.axis_index("tp")
    z, y, core, chip = t // 8, (t // 2) % 4, t % 2, t // 2

    def put_wide(at, value):
        for j in range(value.shape[1] // 128):
            wide[j, at, :] = value[:, j * 128 : (j + 1) * 128]

    def get_wide(at, columns=LANES):
        return jnp.concatenate([wide[j, at, :] for j in range(columns // 128)], axis=1)

    def remote(src, dst, send, recv, device):
        return pltpu.make_async_remote_copy(
            src_ref=src,
            dst_ref=dst,
            send_sem=send,
            recv_sem=recv,
            device_id=device,
            device_id_type=MESH,
        )

    barrier = pltpu.get_barrier_semaphore()

    @pl.loop(1, TP)
    def _(i):
        pl.semaphore_signal(barrier, inc=1, device_id=(x, (t + i) % TP), device_id_type=MESH)

    @pl.loop(1, RING)
    def _(i):
        pl.semaphore_signal(barrier, inc=1, device_id=((x + i) % RING, t), device_id_type=MESH)

    units = hidden.shape[1]

    def columns(own, low, count):
        if low + count <= units:
            return hidden[own, low : low + count].astype(F32)
        rest = hidden[own, low:units].astype(F32)
        return jnp.concatenate(
            [rest, jnp.zeros((rest.shape[0], low + count - units), F32)], axis=1
        )

    for s in range(TP):
        low = s * depth // 128 * 128
        cover = columns(slice(0, HOME), low, LANES + 128)
        cover = pltpu.roll(cover, (LANES + 128 + low - s * depth) % (LANES + 128), 1)
        slabs[s // 2, s % 2 * HOME : (s % 2 + 1) * HOME, :] = cover[:, :LANES].astype(BF16)

    pl.semaphore_wait(barrier, TP - 1 + RING - 1)

    def others(count, me, act):
        @pl.loop(1, count)
        def _(i):
            act((me + i) % count)

    def x_copy(peer, slot):
        return remote(
            slabs.at[peer], xrecv.at[slot], x_send.at[peer], x_recv.at[slot], (x, 2 * peer + core)
        )

    x_own = pltpu.make_async_copy(slabs.at[chip], xrecv.at[chip], local_sem.at[0])
    w_out = remote(weight_in, weight.at[core], w_sem.at[0], w_sem.at[1], (x, t + 1 - 2 * core))
    w_own = pltpu.make_async_copy(weight_in, weight.at[core], local_sem.at[1])

    def base_start():
        others(CHIPS, chip, lambda peer: x_copy(peer, chip).start())
        x_own.start()
        w_out.start()
        w_own.start()

    def base_arrived():
        w_own.wait()
        w_out.wait()
        x_own.wait()
        others(CHIPS, chip, lambda peer: x_copy(peer, peer).wait_recv())

    def running(hit):
        n = hit.shape[0]
        order = lax.broadcasted_iota(jnp.int32, (n, n), 0) >= lax.broadcasted_iota(
            jnp.int32, (n, n), 1
        )
        return jnp.dot(
            order.astype(F32).astype(BF16), hit.astype(BF16), preferred_element_type=F32
        )

    def target(mark, low, count, capacity):
        n = mark.shape[0]
        column = lax.broadcasted_iota(jnp.int32, (n, 128), 1)
        tenants = [(mark == (column + 1 + k).astype(F32)).astype(F32) for k in (0, 128)]
        hit = jnp.dot(
            jnp.concatenate(tenants, axis=1).astype(BF16), places[...], preferred_element_type=F32
        )
        hit = jnp.where((column >= low) & (column < low + count), hit, 0.0)
        slot = (column - low).astype(F32) * capacity + running(hit) - 1.0
        slot = jnp.sum(hit * slot, axis=1, keepdims=True)
        return jnp.where(jnp.sum(hit, axis=1, keepdims=True) > 0, slot, -1.0)

    def set_index(row, slot, empty):
        n = slot.shape[0]
        column = lax.broadcasted_iota(jnp.int32, (n, 128), 1)
        source = lax.broadcasted_iota(jnp.int32, (n, 128), 0)
        back = jnp.where(slot == column.astype(F32), (source - empty).astype(F32), 0.0)
        forth = jnp.where(source == column, jnp.maximum(slot, 0.0), 0.0)
        found[row] = jnp.broadcast_to(
            jnp.sum(back, axis=0, keepdims=True).astype(jnp.int32) + empty, (8, 128)
        )
        found[row + 1] = jnp.broadcast_to(
            jnp.sum(forth, axis=0, keepdims=True).astype(jnp.int32), (8, 128)
        )
        copy = pltpu.make_async_copy(
            found.at[pl.ds(row, 2)], index.at[pl.ds(row, 2)], local_sem.at[12 + row // 2]
        )
        copy.start()
        copy.wait()

    def at_index(row, i, size):
        return jnp.minimum(jnp.maximum(index[row, 0, i], 0), size - 1)

    groups = (group_first, group_second)
    chunks = -(-units // LANES)

    def marks(own):
        return jnp.broadcast_to((tenants[own, :] + 1).astype(F32), (own.stop - own.start, 128))

    def tables_ready():
        device, rank = devices[...].astype(F32), rank_bins[...].astype(F32)
        n = device.shape[1]
        tenant = lax.broadcasted_iota(jnp.int32, (1, n), 1).astype(F32)
        same = lax.broadcasted_iota(jnp.int32, (n, n), 0) == lax.broadcasted_iota(
            jnp.int32, (n, n), 1
        )
        down_device = jnp.sum(jnp.where(same, device, 0.0), axis=1, keepdims=True)
        column = lax.broadcasted_iota(jnp.int32, (n, 128), 1)
        low = jnp.where(column < TP, x * TP + column, (column - TP) * TP).astype(F32)
        span = jnp.where(column < TP, 1, TP).astype(F32)
        places[...] = jnp.where(
            (down_device >= low) & (down_device < low + span), 1.0, 0.0
        ).astype(BF16)

        here = device == (x * TP + t).astype(F32)
        first = jnp.min(jnp.where(here, tenant, float(n)), axis=1, keepdims=True)
        second = jnp.max(jnp.where(here, tenant, -1.0), axis=1, keepdims=True)
        first_rank = jnp.sum(jnp.where(tenant == first, rank, 0.0), axis=1, keepdims=True)
        second_rank = jnp.sum(jnp.where(tenant == second, rank, 0.0), axis=1, keepdims=True)
        wide_shape = (1, gains.shape[1])
        span = lax.broadcasted_iota(jnp.int32, wide_shape, 1).astype(F32)
        gains[0:1, :] = jnp.where(span < first_rank, adapter_scale_fn / jnp.sqrt(first_rank), 0.0)
        gains[1:2, :] = jnp.where(
            (span >= first_rank) & (span < first_rank + second_rank),
            adapter_scale_fn / jnp.sqrt(second_rank),
            0.0,
        )
        gains[2:3, :] = jnp.broadcast_to(first + 1.0, wide_shape)
        gains[3:4, :] = jnp.broadcast_to(second + 1.0, wide_shape)

    def rows_ready():
        few = HOME // 2
        for k in range(2):
            own = slice(k * few, (k + 1) * few)

            for c in range(chunks):
                put_wide(
                    pl.ds(c + c // (PART - 1), few, stride=SLAB_ROWS),
                    columns(own, c * LANES, LANES),
                )
            for c in range(chunks + 1, SLAB_ROWS):
                put_wide(pl.ds(c, few, stride=SLAB_ROWS), jnp.zeros((few, LANES), F32))
            for j in range(LANES // 128):
                wide[j, pl.ds(PART - 1, few, stride=SLAB_ROWS), :] = marks(own)

            @pl.loop(0, few)
            def _(i):
                rows[k * few + i] = get_wide(pl.ds(i * SLAB_ROWS, SLAB_ROWS)).astype(BF16)

        rows[HOME] = jnp.zeros(rows.shape[1:], BF16)

    def a_copy(h, peer, slot):
        return remote(
            packed.at[pl.ds(peer * CAP, CAP), pl.ds(h * PART, PART)],
            groups[h].at[pl.ds(slot * CAP, CAP)],
            a_send.at[h, peer],
            a_recv.at[h, slot],
            (peer, t),
        )

    def a_own(h):
        return pltpu.make_async_copy(
            packed.at[pl.ds(x * CAP, CAP), pl.ds(h * PART, PART)],
            groups[h].at[pl.ds(x * CAP, CAP)],
            local_sem.at[4 + h],
        )

    def group_start():
        set_index(0, target(marks(slice(0, HOME)), TP, RING, CAP), HOME)

        @pl.loop(0, SLOTS)
        def _(i):
            packed[i] = rows[at_index(0, i, HOME + 1)]

        for h in range(2):
            others(RING, x, lambda peer: a_copy(h, peer, x).start())
            a_own(h).start()

    def t_copy(h, peer, slot):
        return remote(
            packed.at[pl.ds(peer * OWN, OWN), pl.ds(h * PART, PART)],
            owned.at[pl.ds(slot * OWN, OWN), pl.ds(h * PART, PART)],
            t_send.at[h, peer],
            t_recv.at[h, slot],
            (x, peer),
        )

    def t_own(h):
        return pltpu.make_async_copy(
            packed.at[pl.ds(t * OWN, OWN), pl.ds(h * PART, PART)],
            owned.at[pl.ds(t * OWN, OWN), pl.ds(h * PART, PART)],
            local_sem.at[6 + h],
        )

    def owner_start(h):
        a_own(h).wait()
        others(RING, x, lambda peer: a_copy(h, peer, peer).wait_recv())
        others(RING, x, lambda peer: a_copy(h, peer, peer).wait_send())

        if h == 0:

            @pl.loop(0, SLOTS)
            def _(i):
                wide[0, pl.ds(i * PART, PART), :] = groups[h][i, :, :128].astype(F32)

            mark = wide[0, pl.ds(PART - 1, SLOTS, stride=PART), :]
            set_index(2, target(mark, 0, TP, OWN), 0)

        @pl.loop(0, SLOTS)
        def _(i):
            packed[i, h * PART : (h + 1) * PART, :] = groups[h][at_index(2, i, SLOTS)]

        others(TP, t, lambda peer: t_copy(h, peer, t).start())
        t_own(h).start()

    def axes(p):
        return (y, z) if p == 0 else (z, y)

    def device(p, a, b):
        return (x, (b * RING + a if p == 0 else a * RING + b) * 2 + core)

    def partial_sum(p, a_to, column):
        b = axes(p)[1]
        total = None
        for k in range(2):
            left = []
            for i in range(RING):
                b_to = (b + i) % RING
                at = b_to * RING + a_to if p == 0 else a_to * RING + b_to
                left.append(xrecv[at, k * HOME : (k + 1) * HOME, :][:, :depth])
            term = jnp.dot(
                jnp.concatenate(left, axis=0),
                weight[k, :, pl.ds(column, TILE)],
                preferred_element_type=F32,
            )
            total = term if total is None else total + term
        return total

    def fill(p, slot, a_to, side, added=None):
        @pl.loop(0, half // TILE)
        def _(n):
            col = pl.multiple_of(n * TILE, TILE)
            total = partial_sum(p, a_to, pl.multiple_of((2 * p + side) * half + n * TILE, TILE))
            if added is not None:
                total = total + relay[p, added, :, pl.ds(col, TILE)].astype(F32)
            parts[p, slot, :, pl.ds(col, TILE)] = total.astype(BF16)

    def r_copy(p, k):
        a, b = axes(p)
        up_to, down_to = device(p, (a + 1) % RING, b), device(p, (a + 3) % RING, b)
        src, dst, to = [
            (0, relay.at[p, 0], up_to),
            (1, relay.at[p, 1], down_to),
            (2, fin_hbm.at[p, 1], up_to),
            (3, fin_hbm.at[p, 2], down_to),
            (0, fin_hbm.at[p, 0], up_to),
            (1, fin_hbm.at[p, 3], down_to),
        ][k]
        return remote(parts.at[p, src], dst, r_send.at[p, k], r_recv.at[p, k], to)

    def reduce_far(p):
        for k in range(2):
            fill(p, k, (axes(p)[0] + 2) % RING, k)
            r_copy(p, k).start()

    def reduce_near(p):
        for k in range(2):
            fill(p, 2 + k, (axes(p)[0] + 1 + 2 * k) % RING, 1 - k)
            r_copy(p, 2 + k).start()

    def reduce_pass(p):
        for k in range(2):
            r_copy(p, k).wait()
            fill(p, k, (axes(p)[0] + 1 + 2 * k) % RING, k, added=k)
            r_copy(p, 4 + k).start()

    def down_copy(s):
        return pltpu.make_async_copy(
            down_in.at[:, pl.ds(pl.multiple_of(s * LANES, LANES), LANES)],
            down.at[s % AHEAD],
            down_sem.at[s % AHEAD],
        )

    tail = (chunks - 1) * LANES
    tail_copy = pltpu.make_async_copy(
        down_in.at[:, tail:units], down_tail, local_sem.at[24]
    )

    def up_copy(s):
        return pltpu.make_async_copy(
            up_in.at[:, pl.ds(pl.multiple_of(s * TILE, TILE), TILE)],
            up.at[s % UP_AHEAD],
            up_sem.at[s % UP_AHEAD],
        )

    def factors_start():
        for s in range(AHEAD):
            down_copy(s).start()
        for s in range(UP_AHEAD):
            up_copy(s).start()
        tail_copy.start()

    def latent_part(h):
        t_own(h).wait()
        others(TP, t, lambda peer: t_copy(h, peer, peer).wait_recv())

        @pl.loop(0, SLOTS)
        def _(i):
            put_wide(
                pl.ds(i * PART, PART), owned[i, h * PART : (h + 1) * PART, :].astype(F32)
            )

        first, last = h * (PART - 1), PART - 1 if h == 0 else chunks

        @pl.loop(0, last - first)
        def _(s):
            piece = get_wide(pl.ds(s, SLOTS, stride=PART)).astype(BF16)
            rows[pl.ds(s * OWN, OWN)] = piece.reshape(OWN, SLAB_ROWS, LANES)

        def term(s, factors):
            left = rows[pl.ds((s - first) * OWN, OWN)].reshape(SLOTS, LANES)
            left = left[:, : factors.shape[1]]
            return lax.dot_general(
                left, factors, (((1,), (1,)), ((), ())), preferred_element_type=F32
            )

        def step(s, total):
            down_copy(s).wait()
            total = total + term(s, down[s % AHEAD])

            @pl.when(s + AHEAD < chunks - 1)
            def _():
                down_copy(s + AHEAD).start()

            return total

        if h == 0:
            mark = get_wide(pl.ds(PART - 1, SLOTS, stride=PART))[:, : latents.shape[1]]
            gain[...] = jnp.where(mark == gains[2:3, :], gains[0:1, :], 0.0) + jnp.where(
                mark == gains[3:4, :], gains[1:2, :], 0.0
            )

        if h == 0:
            start = jnp.zeros(latents.shape, F32)
        else:
            tail_copy.wait()
            start = latents[...] + term(chunks - 1, down_tail[...])
        total = lax.fori_loop(first, min(last, chunks - 1), step, start)
        latents[...] = total if h == 0 else total * gain[...]

    def b_copy(h, peer, slot):
        return remote(
            packed.at[pl.ds(peer * OWN, OWN), pl.ds(h * PART, PART), pl.ds(0, OUT)],
            groups[h].at[pl.ds(slot * OWN, OWN), :, pl.ds(0, OUT)],
            b_send.at[h, peer],
            b_recv.at[h, slot],
            (x, peer),
        )

    def b_own(h):
        return pltpu.make_async_copy(
            packed.at[pl.ds(t * OWN, OWN), pl.ds(h * PART, PART), pl.ds(0, OUT)],
            groups[h].at[pl.ds(t * OWN, OWN), :, pl.ds(0, OUT)],
            local_sem.at[8 + h],
        )

    def back_start(h):
        steps = up_in.shape[1] // TILE
        left = latents[...].astype(BF16)
        others(TP, t, lambda peer: t_copy(h, peer, peer).wait_send())

        @pl.loop(h * steps // 2, (h + 1) * steps // 2)
        def _(s):
            up_copy(s).wait()
            product = jnp.dot(left, up[s % UP_AHEAD], preferred_element_type=F32)
            for j in range(TILE // OUT):
                put_wide(
                    pl.ds((s - h * (steps // 2)) * (TILE // OUT) + j, SLOTS, stride=PART),
                    product[:, j * OUT : (j + 1) * OUT],
                )

            @pl.when(s + UP_AHEAD < steps)
            def _():
                up_copy(s + UP_AHEAD).start()

        @pl.loop(0, SLOTS)
        def _(i):
            packed[i, h * PART : (h + 1) * PART, :OUT] = get_wide(
                pl.ds(i * PART, PART), OUT
            ).astype(BF16)

        others(TP, t, lambda peer: b_copy(h, peer, t).start())
        b_own(h).start()

    def s_copy(p, side, kind):
        a, b = axes(p)
        src, forward = [(1, True), (2 - 2 * side, False), (2 * side, True)][kind]
        step = 1 if forward == (side == 0) else 3
        return remote(
            second_out.at[p, side, src],
            second_in.at[p, side, kind],
            s_send.at[p, side, kind],
            s_recv.at[p, side, kind],
            device(p, a, (b + step) % RING),
        )

    def second_pass(p, side):
        s_copy(p, side, 0).wait()
        held = second_out.at[p, side, 2 * side]
        held[...] = (held[...].astype(F32) + second_in[p, side, 0].astype(F32)).astype(BF16)
        s_copy(p, side, 2).start()

    def reduce_second(p, side):
        came = (4, 3) if side == 0 else (2, 5)
        stage = []
        for i, k in enumerate(came):
            r_copy(p, k).wait_recv()
            slot = side + 2 * i
            stage.append(
                pltpu.make_async_copy(
                    fin_hbm.at[p, slot], parts.at[p, slot], local_sem.at[16 + 4 * p + slot]
                )
            )
        for k in (4 + side, 2 + side):
            r_copy(p, k).wait_send()
        for copy in stage:
            copy.start()
        for copy in stage:
            copy.wait()

        @pl.loop(0, half // TILE)
        def _(n):
            col = pl.multiple_of(n * TILE, TILE)
            at = pl.multiple_of(side * half + n * TILE, TILE)
            total = partial_sum(
                p, axes(p)[0], pl.multiple_of((2 * p + side) * half + n * TILE, TILE)
            )
            total = total + parts[p, side, :, pl.ds(col, TILE)].astype(F32)
            total = total + parts[p, 2 + side, :, pl.ds(col, TILE)].astype(F32)
            own_sum[p, :, pl.ds(at, TILE)] = total[:HOME]
            for d in range(1, RING):
                second_out[p, side, d - 1, :, pl.ds(col, TILE)] = total[
                    d * HOME : (d + 1) * HOME
                ].astype(BF16)

        for kind in range(2):
            s_copy(p, side, kind).start()

    def c_copy(h, peer, slot):
        return remote(
            packed.at[pl.ds(peer * CAP, CAP), pl.ds(h * PART, PART), pl.ds(OUT, OUT)],
            home_in.at[pl.ds(slot * CAP, CAP), pl.ds(h * PART, PART)],
            c_send.at[h, peer],
            c_recv.at[h, slot],
            (peer, t),
        )

    def c_own(h):
        return pltpu.make_async_copy(
            packed.at[pl.ds(x * CAP, CAP), pl.ds(h * PART, PART), pl.ds(OUT, OUT)],
            home_in.at[pl.ds(x * CAP, CAP), pl.ds(h * PART, PART)],
            local_sem.at[10 + h],
        )

    def home_start(h):
        b_own(h).wait()
        others(TP, t, lambda peer: b_copy(h, peer, peer).wait_recv())

        @pl.loop(0, SLOTS)
        def _(i):
            packed[i, h * PART : (h + 1) * PART, OUT:] = groups[h][at_index(3, i, SLOTS)][:, :OUT]

        others(RING, x, lambda peer: c_copy(h, peer, x).start())
        c_own(h).start()

    def second_arrived():
        for p in range(2):
            for side in range(2):
                for kind in range(1, 3):
                    s_copy(p, side, kind).wait()

    def home_arrived(h):
        c_own(h).wait()
        others(RING, x, lambda peer: c_copy(h, peer, peer).wait_recv())

    def finish():
        few = HOME // 2
        for k in range(2):
            own = slice(k * few, (k + 1) * few)

            @pl.loop(0, few)
            def _(i):
                put_wide(pl.ds(i * SLAB_ROWS, SLAB_ROWS), home_in[at_index(1, k * few + i, SLOTS)].astype(F32))

            for p in range(2):
                for side in range(2):

                    @pl.loop(0, PART // 2)
                    def _(n):
                        at = pl.ds(pl.multiple_of(n * OUT, OUT), OUT)
                        column = pl.multiple_of(side * half + n * OUT, OUT)
                        total = own_sum[p, own, pl.ds(column, OUT)]
                        for kind in range(1, 3):
                            total = total + second_in[p, side, kind, own, at].astype(F32)
                        place = p * PART + side * (PART // 2) + n
                        total = total + get_wide(pl.ds(place, few, stride=SLAB_ROWS), OUT)
                        column = pl.multiple_of((2 * p + side) * half + n * OUT, OUT)
                        out[own, pl.ds(column, OUT)] = total.astype(BF16)

    def all_left():
        others(CHIPS, chip, lambda peer: x_copy(peer, peer).wait_send())
        for h in range(2):
            others(TP, t, lambda peer: b_copy(h, peer, peer).wait_send())
            others(RING, x, lambda peer: c_copy(h, peer, peer).wait_send())

    base_start()
    factors_start()
    tables_ready()
    rows_ready()
    group_start()
    owner_start(0)
    base_arrived()
    reduce_far(0)
    owner_start(1)
    reduce_far(1)
    reduce_near(0)
    reduce_near(1)
    latent_part(0)
    reduce_pass(0)
    reduce_pass(1)
    latent_part(1)
    back_start(0)
    back_start(1)
    reduce_second(0, 0)
    reduce_second(1, 0)
    home_start(0)
    reduce_second(0, 1)
    reduce_second(1, 1)
    second_pass(0, 0)
    second_pass(1, 0)
    home_start(1)
    second_pass(0, 1)
    second_pass(1, 1)
    second_arrived()
    home_arrived(0)
    home_arrived(1)
    finish()
    all_left()


def local(
    hidden,
    draft_row_client,
    client_rank_bin,
    client_device,
    down_weight,
    packed_down_factors,
    packed_up_factors,
):
    depth, width = down_weight.shape
    units, rank_columns = packed_down_factors.shape
    tenants = client_rank_bin.shape[0]

    vmem, hbm = pl.BlockSpec(memory_space=pltpu.VMEM), pl.BlockSpec(memory_space=pl.ANY)
    dma = pltpu.SemaphoreType.DMA
    half = width // 4
    out, _ = pl.pallas_call(
        body,
        out_shape=(
            jax.ShapeDtypeStruct((HOME, width), BF16),
            jax.ShapeDtypeStruct((2, 4, RING * HOME, half), BF16),
        ),
        in_specs=[vmem, vmem, vmem, vmem, hbm, hbm, hbm],
        out_specs=(vmem, hbm),
        scratch_shapes=[
            pltpu.VMEM((CHIPS, 2 * HOME, LANES), BF16),
            pltpu.VMEM((HOME + 1, SLAB_ROWS, LANES), BF16),
            pltpu.VMEM((CHIPS, 2 * HOME, LANES), BF16),
            pltpu.VMEM((2, depth, width), BF16),
            pltpu.VMEM((SLOTS, SLAB_ROWS, LANES), BF16),
            pltpu.VMEM((SLOTS, PART, LANES), BF16),
            pltpu.VMEM((SLOTS, PART, LANES), BF16),
            pltpu.VMEM((SLOTS, SLAB_ROWS, LANES), BF16),
            pltpu.VMEM((LANES // 128, SLOTS * PART, 128), F32),
            pltpu.VMEM((AHEAD, rank_columns, LANES), BF16),
            pltpu.VMEM((rank_columns, units % LANES), BF16),
            pltpu.VMEM((UP_AHEAD, rank_columns, TILE), BF16),
            pltpu.VMEM((SLOTS, SLAB_ROWS, OUT), BF16),
            pltpu.VMEM((2, 4, RING * HOME, half), BF16),
            pltpu.VMEM((2, 2, RING * HOME, half), BF16),
            pltpu.VMEM((2, 2, 3, HOME, half), BF16),
            pltpu.VMEM((2, 2, 3, HOME, half), BF16),
            pltpu.VMEM((2, HOME, 2 * half), F32),
            pltpu.VMEM((SLOTS, rank_columns), F32),
            pltpu.VMEM((SLOTS, rank_columns), F32),
            pltpu.VMEM((tenants, 128), BF16),
            pltpu.VMEM((8, rank_columns), F32),
            pltpu.VMEM((4, 8, 128), jnp.int32),
            pltpu.SMEM((4, 8, 128), jnp.int32),
            dma((25,)),
            dma((AHEAD,)),
            dma((UP_AHEAD,)),
            dma((2,)),
            dma((CHIPS,)),
            dma((CHIPS,)),
            dma((2, RING)),
            dma((2, RING)),
            dma((2, TP)),
            dma((2, TP)),
            dma((2, TP)),
            dma((2, TP)),
            dma((2, RING)),
            dma((2, RING)),
            dma((2, 6)),
            dma((2, 6)),
            dma((2, 2, 3)),
            dma((2, 2, 3)),
        ],
        compiler_params=pltpu.CompilerParams(
            collective_id=0, has_side_effects=True, vmem_limit_bytes=63 << 20
        ),
        name="verify_rows",
    )(
        draft_row_client.reshape(HOME, 1),
        client_rank_bin.reshape(1, tenants),
        client_device.reshape(1, tenants),
        hidden,
        down_weight,
        packed_down_factors.T,
        packed_up_factors,
    )
    return out


def solution(mesh):
    placed = (
        P(("dp", "tp"), None),
        P(("dp", "tp")),
        P(),
        P(),
        P("tp", None),
        P(None, ("dp", "tp")),
        P(("dp", "tp"), None),
    )
    return jax.shard_map(
        local, mesh=mesh, in_specs=placed, out_specs=P(("dp", "tp"), None), check_vma=False
    )
```

```python
import functools

import jax
import jax.numpy as jnp
from jax import lax
from jax.experimental import pallas as pl
from jax.experimental.pallas import tpu as pltpu
from jax.sharding import PartitionSpec as P

MESH = pl.DeviceIdType.MESH
BF16 = jnp.bfloat16
F32 = jnp.float32
adapter_scale_fn = 4.0

RING = 4
CHIPS = RING * RING
TP = 2 * CHIPS
HOME = 64
CAP = 24
OWN = 3
SLOTS = RING * CAP
LANES = 512
TILE = 512
SLAB_ROWS = TP
PART = SLAB_ROWS // 2
OUT = 256
AHEAD = 8
UP_AHEAD = 4


def body(
    tenants,
    rank_bins,
    devices,
    hidden,
    weight_in,
    down_in,
    up_in,
    out,
    fin_hbm,
    slabs,
    rows,
    xrecv,
    weight,
    packed,
    group_first,
    group_second,
    owned,
    wide,
    down,
    down_tail,
    up,
    home_in,
    parts,
    relay,
    second_out,
    second_in,
    own_sum,
    latents,
    gain,
    places,
    gains,
    found,
    index,
    local_sem,
    down_sem,
    up_sem,
    w_sem,
    x_send,
    x_recv,
    a_send,
    a_recv,
    t_send,
    t_recv,
    b_send,
    b_recv,
    c_send,
    c_recv,
    r_send,
    r_recv,
    s_send,
    s_recv,
):
    width = weight.shape[2]
    depth = weight.shape[1]
    half = width // 4
    x, t = lax.axis_index("dp"), lax.axis_index("tp")
    z, y, core, chip = t // 8, (t // 2) % 4, t % 2, t // 2

    def put_wide(at, value):
        for j in range(value.shape[1] // 128):
            wide[j, at, :] = value[:, j * 128 : (j + 1) * 128]

    def get_wide(at, columns=LANES):
        return jnp.concatenate([wide[j, at, :] for j in range(columns // 128)], axis=1)

    def remote(src, dst, send, recv, device):
        return pltpu.make_async_remote_copy(
            src_ref=src,
            dst_ref=dst,
            send_sem=send,
            recv_sem=recv,
            device_id=device,
            device_id_type=MESH,
        )

    barrier = pltpu.get_barrier_semaphore()

    @pl.loop(1, TP)
    def _(i):
        pl.semaphore_signal(barrier, inc=1, device_id=(x, (t + i) % TP), device_id_type=MESH)

    @pl.loop(1, RING)
    def _(i):
        pl.semaphore_signal(barrier, inc=1, device_id=((x + i) % RING, t), device_id_type=MESH)

    units = hidden.shape[1]

    def columns(own, low, count):
        if low + count <= units:
            return hidden[own, low : low + count].astype(F32)
        rest = hidden[own, low:units].astype(F32)
        return jnp.concatenate(
            [rest, jnp.zeros((rest.shape[0], low + count - units), F32)], axis=1
        )

    for s in range(TP):
        low = s * depth // 128 * 128
        cover = columns(slice(0, HOME), low, LANES + 128)
        cover = pltpu.roll(cover, (LANES + 128 + low - s * depth) % (LANES + 128), 1)
        slabs[s // 2, s % 2 * HOME : (s % 2 + 1) * HOME, :] = cover[:, :LANES].astype(BF16)

    pl.semaphore_wait(barrier, TP - 1 + RING - 1)

    def others(count, me, act):
        @pl.loop(1, count)
        def _(i):
            act((me + i) % count)

    def x_copy(peer, slot):
        return remote(
            slabs.at[peer], xrecv.at[slot], x_send.at[peer], x_recv.at[slot], (x, 2 * peer + core)
        )

    x_own = pltpu.make_async_copy(slabs.at[chip], xrecv.at[chip], local_sem.at[0])
    w_out = remote(weight_in, weight.at[core], w_sem.at[0], w_sem.at[1], (x, t + 1 - 2 * core))
    w_own = pltpu.make_async_copy(weight_in, weight.at[core], local_sem.at[1])

    def base_start():
        others(CHIPS, chip, lambda peer: x_copy(peer, chip).start())
        x_own.start()
        w_out.start()
        w_own.start()

    def base_arrived():
        w_own.wait()
        w_out.wait()
        x_own.wait()
        others(CHIPS, chip, lambda peer: x_copy(peer, peer).wait_recv())

    def running(hit):
        n = hit.shape[0]
        order = lax.broadcasted_iota(jnp.int32, (n, n), 0) >= lax.broadcasted_iota(
            jnp.int32, (n, n), 1
        )
        return jnp.dot(
            order.astype(F32).astype(BF16), hit.astype(BF16), preferred_element_type=F32
        )

    def target(mark, low, count, capacity):
        n = mark.shape[0]
        column = lax.broadcasted_iota(jnp.int32, (n, 128), 1)
        tenants = [(mark == (column + 1 + k).astype(F32)).astype(F32) for k in (0, 128)]
        hit = jnp.dot(
            jnp.concatenate(tenants, axis=1).astype(BF16), places[...], preferred_element_type=F32
        )
        hit = jnp.where((column >= low) & (column < low + count), hit, 0.0)
        slot = (column - low).astype(F32) * capacity + running(hit) - 1.0
        slot = jnp.sum(hit * slot, axis=1, keepdims=True)
        return jnp.where(jnp.sum(hit, axis=1, keepdims=True) > 0, slot, -1.0)

    def set_index(row, slot, empty):
        n = slot.shape[0]
        column = lax.broadcasted_iota(jnp.int32, (n, 128), 1)
        source = lax.broadcasted_iota(jnp.int32, (n, 128), 0)
        back = jnp.where(slot == column.astype(F32), (source - empty).astype(F32), 0.0)
        forth = jnp.where(source == column, jnp.maximum(slot, 0.0), 0.0)
        found[row] = jnp.broadcast_to(
            jnp.sum(back, axis=0, keepdims=True).astype(jnp.int32) + empty, (8, 128)
        )
        found[row + 1] = jnp.broadcast_to(
            jnp.sum(forth, axis=0, keepdims=True).astype(jnp.int32), (8, 128)
        )
        copy = pltpu.make_async_copy(
            found.at[pl.ds(row, 2)], index.at[pl.ds(row, 2)], local_sem.at[12 + row // 2]
        )
        copy.start()
        copy.wait()

    def at_index(row, i, size):
        return jnp.minimum(jnp.maximum(index[row, 0, i], 0), size - 1)

    groups = (group_first, group_second)
    chunks = -(-units // LANES)

    def marks(own):
        few = own.stop - own.start
        row = jnp.broadcast_to((tenants[...] + 1).astype(F32), (few, HOME))
        same = lax.broadcasted_iota(jnp.int32, (few, HOME), 0) + own.start
        same = same == lax.broadcasted_iota(jnp.int32, (few, HOME), 1)
        column = jnp.sum(jnp.where(same, row, 0.0), axis=1, keepdims=True)
        return jnp.broadcast_to(column, (few, 128))

    def tables_ready():
        device, rank = devices[...].astype(F32), rank_bins[...].astype(F32)
        n = device.shape[1]
        tenant = lax.broadcasted_iota(jnp.int32, (1, n), 1).astype(F32)
        same = lax.broadcasted_iota(jnp.int32, (n, n), 0) == lax.broadcasted_iota(
            jnp.int32, (n, n), 1
        )
        down_device = jnp.sum(jnp.where(same, device, 0.0), axis=1, keepdims=True)
        column = lax.broadcasted_iota(jnp.int32, (n, 128), 1)
        low = jnp.where(column < TP, x * TP + column, (column - TP) * TP).astype(F32)
        span = jnp.where(column < TP, 1, TP).astype(F32)
        places[...] = jnp.where(
            (down_device >= low) & (down_device < low + span), 1.0, 0.0
        ).astype(BF16)

        here = device == (x * TP + t).astype(F32)
        first = jnp.min(jnp.where(here, tenant, float(n)), axis=1, keepdims=True)
        second = jnp.max(jnp.where(here, tenant, -1.0), axis=1, keepdims=True)
        first_rank = jnp.sum(jnp.where(tenant == first, rank, 0.0), axis=1, keepdims=True)
        second_rank = jnp.sum(jnp.where(tenant == second, rank, 0.0), axis=1, keepdims=True)
        wide_shape = (1, gains.shape[1])
        span = lax.broadcasted_iota(jnp.int32, wide_shape, 1).astype(F32)
        gains[0:1, :] = jnp.where(span < first_rank, adapter_scale_fn / jnp.sqrt(first_rank), 0.0)
        gains[1:2, :] = jnp.where(
            (span >= first_rank) & (span < first_rank + second_rank),
            adapter_scale_fn / jnp.sqrt(second_rank),
            0.0,
        )
        gains[2:3, :] = jnp.broadcast_to(first + 1.0, wide_shape)
        gains[3:4, :] = jnp.broadcast_to(second + 1.0, wide_shape)

    def rows_ready():
        few = HOME // 2
        for k in range(2):
            own = slice(k * few, (k + 1) * few)

            for c in range(chunks):
                put_wide(
                    pl.ds(c + c // (PART - 1), few, stride=SLAB_ROWS),
                    columns(own, c * LANES, LANES),
                )
            for c in range(chunks + 1, SLAB_ROWS):
                put_wide(pl.ds(c, few, stride=SLAB_ROWS), jnp.zeros((few, LANES), F32))
            for j in range(LANES // 128):
                wide[j, pl.ds(PART - 1, few, stride=SLAB_ROWS), :] = marks(own)

            @pl.loop(0, few)
            def _(i):
                rows[k * few + i] = get_wide(pl.ds(i * SLAB_ROWS, SLAB_ROWS)).astype(BF16)

        rows[HOME] = jnp.zeros(rows.shape[1:], BF16)

    def a_copy(h, peer, slot):
        return remote(
            packed.at[pl.ds(peer * CAP, CAP), pl.ds(h * PART, PART)],
            groups[h].at[pl.ds(slot * CAP, CAP)],
            a_send.at[h, peer],
            a_recv.at[h, slot],
            (peer, t),
        )

    def a_own(h):
        return pltpu.make_async_copy(
            packed.at[pl.ds(x * CAP, CAP), pl.ds(h * PART, PART)],
            groups[h].at[pl.ds(x * CAP, CAP)],
            local_sem.at[4 + h],
        )

    def group_start():
        set_index(0, target(marks(slice(0, HOME)), TP, RING, CAP), HOME)

        @pl.loop(0, SLOTS)
        def _(i):
            packed[i] = rows[at_index(0, i, HOME + 1)]

        for h in range(2):
            others(RING, x, lambda peer: a_copy(h, peer, x).start())
            a_own(h).start()

    def t_copy(h, peer, slot):
        return remote(
            packed.at[pl.ds(peer * OWN, OWN), pl.ds(h * PART, PART)],
            owned.at[pl.ds(slot * OWN, OWN), pl.ds(h * PART, PART)],
            t_send.at[h, peer],
            t_recv.at[h, slot],
            (x, peer),
        )

    def t_own(h):
        return pltpu.make_async_copy(
            packed.at[pl.ds(t * OWN, OWN), pl.ds(h * PART, PART)],
            owned.at[pl.ds(t * OWN, OWN), pl.ds(h * PART, PART)],
            local_sem.at[6 + h],
        )

    def owner_start(h):
        a_own(h).wait()
        others(RING, x, lambda peer: a_copy(h, peer, peer).wait_recv())
        others(RING, x, lambda peer: a_copy(h, peer, peer).wait_send())

        if h == 0:

            @pl.loop(0, SLOTS)
            def _(i):
                wide[0, pl.ds(i * PART, PART), :] = groups[h][i, :, :128].astype(F32)

            mark = wide[0, pl.ds(PART - 1, SLOTS, stride=PART), :]
            set_index(2, target(mark, 0, TP, OWN), 0)

        @pl.loop(0, SLOTS)
        def _(i):
            packed[i, h * PART : (h + 1) * PART, :] = groups[h][at_index(2, i, SLOTS)]

        others(TP, t, lambda peer: t_copy(h, peer, t).start())
        t_own(h).start()

    def axes(p):
        return (y, z) if p == 0 else (z, y)

    def device(p, a, b):
        return (x, (b * RING + a if p == 0 else a * RING + b) * 2 + core)

    def partial_sum(p, a_to, column):
        b = axes(p)[1]
        total = None
        for k in range(2):
            left = []
            for i in range(RING):
                b_to = (b + i) % RING
                at = b_to * RING + a_to if p == 0 else a_to * RING + b_to
                left.append(xrecv[at, k * HOME : (k + 1) * HOME, :][:, :depth])
            term = jnp.dot(
                jnp.concatenate(left, axis=0),
                weight[k, :, pl.ds(column, TILE)],
                preferred_element_type=F32,
            )
            total = term if total is None else total + term
        return total

    def fill(p, slot, a_to, side, added=None):
        @pl.loop(0, half // TILE)
        def _(n):
            col = pl.multiple_of(n * TILE, TILE)
            total = partial_sum(p, a_to, pl.multiple_of((2 * p + side) * half + n * TILE, TILE))
            if added is not None:
                total = total + relay[p, added, :, pl.ds(col, TILE)].astype(F32)
            parts[p, slot, :, pl.ds(col, TILE)] = total.astype(BF16)

    def r_copy(p, k):
        a, b = axes(p)
        up_to, down_to = device(p, (a + 1) % RING, b), device(p, (a + 3) % RING, b)
        src, dst, to = [
            (0, relay.at[p, 0], up_to),
            (1, relay.at[p, 1], down_to),
            (2, fin_hbm.at[p, 1], up_to),
            (3, fin_hbm.at[p, 2], down_to),
            (0, fin_hbm.at[p, 0], up_to),
            (1, fin_hbm.at[p, 3], down_to),
        ][k]
        return remote(parts.at[p, src], dst, r_send.at[p, k], r_recv.at[p, k], to)

    def reduce_far(p, k):
        fill(p, k, (axes(p)[0] + 2) % RING, k)
        r_copy(p, k).start()

    def reduce_near(p, k):
        fill(p, 2 + k, (axes(p)[0] + 1 + 2 * k) % RING, 1 - k)
        r_copy(p, 2 + k).start()

    def reduce_pass(p, k):
        r_copy(p, k).wait()
        fill(p, k, (axes(p)[0] + 1 + 2 * k) % RING, k, added=k)
        r_copy(p, 4 + k).start()

    def down_copy(s):
        return pltpu.make_async_copy(
            down_in.at[:, pl.ds(pl.multiple_of(s * LANES, LANES), LANES)],
            down.at[s % AHEAD],
            down_sem.at[s % AHEAD],
        )

    tail = (chunks - 1) * LANES
    tail_copy = pltpu.make_async_copy(
        down_in.at[:, tail:units], down_tail, local_sem.at[24]
    )

    def up_copy(s):
        return pltpu.make_async_copy(
            up_in.at[:, pl.ds(pl.multiple_of(s * TILE, TILE), TILE)],
            up.at[s % UP_AHEAD],
            up_sem.at[s % UP_AHEAD],
        )

    def factors_start():
        for s in range(AHEAD):
            down_copy(s).start()
        for s in range(UP_AHEAD):
            up_copy(s).start()
        tail_copy.start()

    def latent_part(h):
        t_own(h).wait()
        others(TP, t, lambda peer: t_copy(h, peer, peer).wait_recv())

        @pl.loop(0, SLOTS)
        def _(i):
            put_wide(
                pl.ds(i * PART, PART), owned[i, h * PART : (h + 1) * PART, :].astype(F32)
            )

        first, last = h * (PART - 1), PART - 1 if h == 0 else chunks

        @pl.loop(0, last - first)
        def _(s):
            piece = get_wide(pl.ds(s, SLOTS, stride=PART)).astype(BF16)
            rows[pl.ds(s * OWN, OWN)] = piece.reshape(OWN, SLAB_ROWS, LANES)

        def term(s, factors):
            left = rows[pl.ds((s - first) * OWN, OWN)].reshape(SLOTS, LANES)
            left = left[:, : factors.shape[1]]
            return lax.dot_general(
                left, factors, (((1,), (1,)), ((), ())), preferred_element_type=F32
            )

        def step(s, total):
            down_copy(s).wait()
            total = total + term(s, down[s % AHEAD])

            @pl.when(s + AHEAD < chunks - 1)
            def _():
                down_copy(s + AHEAD).start()

            return total

        if h == 0:
            mark = get_wide(pl.ds(PART - 1, SLOTS, stride=PART))[:, : latents.shape[1]]
            gain[...] = jnp.where(mark == gains[2:3, :], gains[0:1, :], 0.0) + jnp.where(
                mark == gains[3:4, :], gains[1:2, :], 0.0
            )

        if h == 0:
            start = jnp.zeros(latents.shape, F32)
        else:
            tail_copy.wait()
            start = latents[...] + term(chunks - 1, down_tail[...])
        total = lax.fori_loop(first, min(last, chunks - 1), step, start)
        latents[...] = total if h == 0 else total * gain[...]

    def b_copy(h, peer, slot):
        return remote(
            packed.at[pl.ds(peer * OWN, OWN), pl.ds(h * PART, PART), pl.ds(0, OUT)],
            groups[h].at[pl.ds(slot * OWN, OWN), :, pl.ds(0, OUT)],
            b_send.at[h, peer],
            b_recv.at[h, slot],
            (x, peer),
        )

    def b_own(h):
        return pltpu.make_async_copy(
            packed.at[pl.ds(t * OWN, OWN), pl.ds(h * PART, PART), pl.ds(0, OUT)],
            groups[h].at[pl.ds(t * OWN, OWN), :, pl.ds(0, OUT)],
            local_sem.at[8 + h],
        )

    def back_start(h):
        steps = up_in.shape[1] // TILE
        left = latents[...].astype(BF16)
        others(TP, t, lambda peer: t_copy(h, peer, peer).wait_send())

        @pl.loop(h * steps // 2, (h + 1) * steps // 2)
        def _(s):
            up_copy(s).wait()
            product = jnp.dot(left, up[s % UP_AHEAD], preferred_element_type=F32)
            for j in range(TILE // OUT):
                put_wide(
                    pl.ds((s - h * (steps // 2)) * (TILE // OUT) + j, SLOTS, stride=PART),
                    product[:, j * OUT : (j + 1) * OUT],
                )

            @pl.when(s + UP_AHEAD < steps)
            def _():
                up_copy(s + UP_AHEAD).start()

        @pl.loop(0, SLOTS)
        def _(i):
            packed[i, h * PART : (h + 1) * PART, :OUT] = get_wide(
                pl.ds(i * PART, PART), OUT
            ).astype(BF16)

        others(TP, t, lambda peer: b_copy(h, peer, t).start())
        b_own(h).start()

    def s_copy(p, side, kind):
        a, b = axes(p)
        src, forward = [(1, True), (2 - 2 * side, False), (2 * side, True)][kind]
        step = 1 if forward == (side == 0) else 3
        return remote(
            second_out.at[p, side, src],
            second_in.at[p, side, kind],
            s_send.at[p, side, kind],
            s_recv.at[p, side, kind],
            device(p, a, (b + step) % RING),
        )

    def second_pass(p, side):
        s_copy(p, side, 0).wait()
        held = second_out.at[p, side, 2 * side]
        held[...] = (held[...].astype(F32) + second_in[p, side, 0].astype(F32)).astype(BF16)
        s_copy(p, side, 2).start()

    def reduce_second(p, side):
        came = (4, 3) if side == 0 else (2, 5)
        stage = []
        for i, k in enumerate(came):
            r_copy(p, k).wait_recv()
            slot = side + 2 * i
            stage.append(
                pltpu.make_async_copy(
                    fin_hbm.at[p, slot], parts.at[p, slot], local_sem.at[16 + 4 * p + slot]
                )
            )
        for k in (4 + side, 2 + side):
            r_copy(p, k).wait_send()
        for copy in stage:
            copy.start()
        for copy in stage:
            copy.wait()

        @pl.loop(0, half // TILE)
        def _(n):
            col = pl.multiple_of(n * TILE, TILE)
            at = pl.multiple_of(side * half + n * TILE, TILE)
            total = partial_sum(
                p, axes(p)[0], pl.multiple_of((2 * p + side) * half + n * TILE, TILE)
            )
            total = total + parts[p, side, :, pl.ds(col, TILE)].astype(F32)
            total = total + parts[p, 2 + side, :, pl.ds(col, TILE)].astype(F32)
            own_sum[p, :, pl.ds(at, TILE)] = total[:HOME]
            for d in range(1, RING):
                second_out[p, side, d - 1, :, pl.ds(col, TILE)] = total[
                    d * HOME : (d + 1) * HOME
                ].astype(BF16)

        for kind in range(2):
            s_copy(p, side, kind).start()

    def c_copy(h, peer, slot):
        return remote(
            packed.at[pl.ds(peer * CAP, CAP), pl.ds(h * PART, PART), pl.ds(OUT, OUT)],
            home_in.at[pl.ds(slot * CAP, CAP), pl.ds(h * PART, PART)],
            c_send.at[h, peer],
            c_recv.at[h, slot],
            (peer, t),
        )

    def c_own(h):
        return pltpu.make_async_copy(
            packed.at[pl.ds(x * CAP, CAP), pl.ds(h * PART, PART), pl.ds(OUT, OUT)],
            home_in.at[pl.ds(x * CAP, CAP), pl.ds(h * PART, PART)],
            local_sem.at[10 + h],
        )

    def home_start(h):
        b_own(h).wait()
        others(TP, t, lambda peer: b_copy(h, peer, peer).wait_recv())

        @pl.loop(0, SLOTS)
        def _(i):
            packed[i, h * PART : (h + 1) * PART, OUT:] = groups[h][at_index(3, i, SLOTS)][:, :OUT]

        others(RING, x, lambda peer: c_copy(h, peer, x).start())
        c_own(h).start()

    def second_arrived():
        for p in range(2):
            for side in range(2):
                for kind in range(1, 3):
                    s_copy(p, side, kind).wait()

                @pl.loop(0, half // TILE)
                def _(n):
                    at = pl.ds(pl.multiple_of(n * TILE, TILE), TILE)
                    column = pl.ds(pl.multiple_of(side * half + n * TILE, TILE), TILE)
                    total = own_sum[p, :, column]
                    for kind in range(1, 3):
                        total = total + second_in[p, side, kind, :, at].astype(F32)
                    own_sum[p, :, column] = total

    def home_arrived(h):
        c_own(h).wait()
        others(RING, x, lambda peer: c_copy(h, peer, peer).wait_recv())

    def finish():
        few = HOME // 2
        for k in range(2):
            own = slice(k * few, (k + 1) * few)

            @pl.loop(0, few)
            def _(i):
                put_wide(pl.ds(i * SLAB_ROWS, SLAB_ROWS), home_in[at_index(1, k * few + i, SLOTS)].astype(F32))

            @pl.loop(0, SLAB_ROWS)
            def _(n):
                column = pl.multiple_of(n * OUT, OUT)
                at = pl.ds(pl.multiple_of(n % PART * OUT, OUT), OUT)
                total = own_sum[n // PART, own, at]
                total = total + get_wide(pl.ds(n, few, stride=SLAB_ROWS), OUT)
                out[own, pl.ds(column, OUT)] = total.astype(BF16)

    def all_left():
        others(CHIPS, chip, lambda peer: x_copy(peer, peer).wait_send())
        for h in range(2):
            others(TP, t, lambda peer: b_copy(h, peer, peer).wait_send())
            others(RING, x, lambda peer: c_copy(h, peer, peer).wait_send())

    base_start()
    factors_start()
    tables_ready()
    rows_ready()
    group_start()
    owner_start(0)
    base_arrived()
    reduce_far(0, 0)
    reduce_far(1, 0)
    reduce_far(0, 1)
    reduce_far(1, 1)
    reduce_near(0, 0)
    reduce_near(1, 0)
    owner_start(1)
    reduce_near(0, 1)
    reduce_near(1, 1)
    reduce_pass(0, 0)
    reduce_pass(1, 0)
    latent_part(0)
    reduce_pass(0, 1)
    reduce_pass(1, 1)
    latent_part(1)
    back_start(0)
    back_start(1)
    reduce_second(0, 0)
    reduce_second(1, 0)
    reduce_second(0, 1)
    reduce_second(1, 1)
    home_start(0)
    second_pass(0, 0)
    second_pass(1, 0)
    home_start(1)
    second_pass(0, 1)
    second_pass(1, 1)
    second_arrived()
    home_arrived(0)
    home_arrived(1)
    finish()
    all_left()


def local(
    hidden,
    draft_row_client,
    client_rank_bin,
    client_device,
    down_weight,
    packed_down_factors,
    packed_up_factors,
):
    depth, width = down_weight.shape
    units, rank_columns = packed_down_factors.shape
    tenants = client_rank_bin.shape[0]

    vmem, hbm = pl.BlockSpec(memory_space=pltpu.VMEM), pl.BlockSpec(memory_space=pl.ANY)
    dma = pltpu.SemaphoreType.DMA
    half = width // 4
    out, _ = pl.pallas_call(
        body,
        out_shape=(
            jax.ShapeDtypeStruct((HOME, width), BF16),
            jax.ShapeDtypeStruct((2, 4, RING * HOME, half), BF16),
        ),
        in_specs=[vmem, vmem, vmem, vmem, hbm, hbm, hbm],
        out_specs=(vmem, hbm),
        scratch_shapes=[
            pltpu.VMEM((CHIPS, 2 * HOME, LANES), BF16),
            pltpu.VMEM((HOME + 1, SLAB_ROWS, LANES), BF16),
            pltpu.VMEM((CHIPS, 2 * HOME, LANES), BF16),
            pltpu.VMEM((2, depth, width), BF16),
            pltpu.VMEM((SLOTS, SLAB_ROWS, LANES), BF16),
            pltpu.VMEM((SLOTS, PART, LANES), BF16),
            pltpu.VMEM((SLOTS, PART, LANES), BF16),
            pltpu.VMEM((SLOTS, SLAB_ROWS, LANES), BF16),
            pltpu.VMEM((LANES // 128, SLOTS * PART, 128), F32),
            pltpu.VMEM((AHEAD, rank_columns, LANES), BF16),
            pltpu.VMEM((rank_columns, units % LANES), BF16),
            pltpu.VMEM((UP_AHEAD, rank_columns, TILE), BF16),
            pltpu.VMEM((SLOTS, SLAB_ROWS, OUT), BF16),
            pltpu.VMEM((2, 4, RING * HOME, half), BF16),
            pltpu.VMEM((2, 2, RING * HOME, half), BF16),
            pltpu.VMEM((2, 2, 3, HOME, half), BF16),
            pltpu.VMEM((2, 2, 3, HOME, half), BF16),
            pltpu.VMEM((2, HOME, 2 * half), F32),
            pltpu.VMEM((SLOTS, rank_columns), F32),
            pltpu.VMEM((SLOTS, rank_columns), F32),
            pltpu.VMEM((tenants, 128), BF16),
            pltpu.VMEM((8, rank_columns), F32),
            pltpu.VMEM((4, 8, 128), jnp.int32),
            pltpu.SMEM((4, 8, 128), jnp.int32),
            dma((25,)),
            dma((AHEAD,)),
            dma((UP_AHEAD,)),
            dma((2,)),
            dma((CHIPS,)),
            dma((CHIPS,)),
            dma((2, RING)),
            dma((2, RING)),
            dma((2, TP)),
            dma((2, TP)),
            dma((2, TP)),
            dma((2, TP)),
            dma((2, RING)),
            dma((2, RING)),
            dma((2, 6)),
            dma((2, 6)),
            dma((2, 2, 3)),
            dma((2, 2, 3)),
        ],
        compiler_params=pltpu.CompilerParams(
            collective_id=0, has_side_effects=True, vmem_limit_bytes=63 << 20
        ),
        name="verify_rows",
    )(
        draft_row_client.reshape(1, HOME),
        client_rank_bin.reshape(1, tenants),
        client_device.reshape(1, tenants),
        hidden,
        down_weight,
        packed_down_factors.T,
        packed_up_factors,
    )
    return out


def solution(mesh):
    placed = (
        P(("dp", "tp"), None),
        P(("dp", "tp")),
        P(),
        P(),
        P("tp", None),
        P(None, ("dp", "tp")),
        P(("dp", "tp"), None),
    )
    return jax.shard_map(
        local, mesh=mesh, in_specs=placed, out_specs=P(("dp", "tp"), None), check_vma=False
    )
```

```python
import functools

import jax
import jax.numpy as jnp
from jax import lax
from jax.experimental import pallas as pl
from jax.experimental.pallas import tpu as pltpu
from jax.sharding import PartitionSpec as P

MESH = pl.DeviceIdType.MESH
BF16 = jnp.bfloat16
F32 = jnp.float32
adapter_scale_fn = 4.0

RING = 4
CHIPS = RING * RING
TP = 2 * CHIPS
HOME = 64
CAP = 24
OWN = 3
SLOTS = RING * CAP
LANES = 512
TILE = 512
SLAB_ROWS = TP
PART = SLAB_ROWS // 2
OUT = 256
AHEAD = 8
UP_AHEAD = 4


def body(
    tenants,
    rank_bins,
    devices,
    hidden,
    weight_in,
    down_in,
    up_in,
    out,
    fin_hbm,
    slabs,
    rows,
    xrecv,
    weight,
    packed,
    group_first,
    group_second,
    owned,
    wide,
    down,
    down_tail,
    up,
    home_in,
    parts,
    relay,
    second_out,
    second_in,
    own_sum,
    latents,
    gain,
    places,
    gains,
    found,
    index,
    local_sem,
    down_sem,
    up_sem,
    w_sem,
    x_send,
    x_recv,
    a_send,
    a_recv,
    t_send,
    t_recv,
    b_send,
    b_recv,
    c_send,
    c_recv,
    r_send,
    r_recv,
    s_send,
    s_recv,
):
    width = weight.shape[2]
    depth = weight.shape[1]
    half = width // 4
    x, t = lax.axis_index("dp"), lax.axis_index("tp")
    z, y, core, chip = t // 8, (t // 2) % 4, t % 2, t // 2

    def put_wide(at, value):
        for j in range(value.shape[1] // 128):
            wide[j, at, :] = value[:, j * 128 : (j + 1) * 128]

    def get_wide(at, columns=LANES):
        return jnp.concatenate([wide[j, at, :] for j in range(columns // 128)], axis=1)

    def remote(src, dst, send, recv, device):
        return pltpu.make_async_remote_copy(
            src_ref=src,
            dst_ref=dst,
            send_sem=send,
            recv_sem=recv,
            device_id=device,
            device_id_type=MESH,
        )

    barrier = pltpu.get_barrier_semaphore()

    @pl.loop(1, TP)
    def _(i):
        pl.semaphore_signal(barrier, inc=1, device_id=(x, (t + i) % TP), device_id_type=MESH)

    @pl.loop(1, RING)
    def _(i):
        pl.semaphore_signal(barrier, inc=1, device_id=((x + i) % RING, t), device_id_type=MESH)

    units = hidden.shape[1]

    def columns(own, low, count):
        if low + count <= units:
            return hidden[own, low : low + count].astype(F32)
        rest = hidden[own, low:units].astype(F32)
        return jnp.concatenate(
            [rest, jnp.zeros((rest.shape[0], low + count - units), F32)], axis=1
        )

    for s in range(TP):
        low = s * depth // 128 * 128
        cover = columns(slice(0, HOME), low, LANES + 128)
        cover = pltpu.roll(cover, (LANES + 128 + low - s * depth) % (LANES + 128), 1)
        slabs[s // 2, s % 2 * HOME : (s % 2 + 1) * HOME, :] = cover[:, :LANES].astype(BF16)

    pl.semaphore_wait(barrier, TP - 1 + RING - 1)

    def others(count, me, act):
        @pl.loop(1, count)
        def _(i):
            act((me + i) % count)

    def x_copy(peer, slot):
        return remote(
            slabs.at[peer], xrecv.at[slot], x_send.at[peer], x_recv.at[slot], (x, 2 * peer + core)
        )

    x_own = pltpu.make_async_copy(slabs.at[chip], xrecv.at[chip], local_sem.at[0])
    w_out = remote(weight_in, weight.at[core], w_sem.at[0], w_sem.at[1], (x, t + 1 - 2 * core))
    w_own = pltpu.make_async_copy(weight_in, weight.at[core], local_sem.at[1])

    def base_start():
        others(CHIPS, chip, lambda peer: x_copy(peer, chip).start())
        x_own.start()
        w_out.start()
        w_own.start()

    def base_arrived():
        w_own.wait()
        w_out.wait()
        x_own.wait()
        others(CHIPS, chip, lambda peer: x_copy(peer, peer).wait_recv())

    def running(hit):
        n = hit.shape[0]
        order = lax.broadcasted_iota(jnp.int32, (n, n), 0) >= lax.broadcasted_iota(
            jnp.int32, (n, n), 1
        )
        return jnp.dot(
            order.astype(F32).astype(BF16), hit.astype(BF16), preferred_element_type=F32
        )

    def target(mark, low, count, capacity):
        n = mark.shape[0]
        column = lax.broadcasted_iota(jnp.int32, (n, 128), 1)
        tenants = [(mark == (column + 1 + k).astype(F32)).astype(F32) for k in (0, 128)]
        hit = jnp.dot(
            jnp.concatenate(tenants, axis=1).astype(BF16), places[...], preferred_element_type=F32
        )
        hit = jnp.where((column >= low) & (column < low + count), hit, 0.0)
        slot = (column - low).astype(F32) * capacity + running(hit) - 1.0
        slot = jnp.sum(hit * slot, axis=1, keepdims=True)
        return jnp.where(jnp.sum(hit, axis=1, keepdims=True) > 0, slot, -1.0)

    def set_index(row, slot, empty):
        n = slot.shape[0]
        column = lax.broadcasted_iota(jnp.int32, (n, 128), 1)
        source = lax.broadcasted_iota(jnp.int32, (n, 128), 0)
        back = jnp.where(slot == column.astype(F32), (source - empty).astype(F32), 0.0)
        forth = jnp.where(source == column, jnp.maximum(slot, 0.0), 0.0)
        found[row] = jnp.broadcast_to(
            jnp.sum(back, axis=0, keepdims=True).astype(jnp.int32) + empty, (8, 128)
        )
        found[row + 1] = jnp.broadcast_to(
            jnp.sum(forth, axis=0, keepdims=True).astype(jnp.int32), (8, 128)
        )
        copy = pltpu.make_async_copy(
            found.at[pl.ds(row, 2)], index.at[pl.ds(row, 2)], local_sem.at[12 + row // 2]
        )
        copy.start()
        copy.wait()

    def at_index(row, i, size):
        return jnp.minimum(jnp.maximum(index[row, 0, i], 0), size - 1)

    groups = (group_first, group_second)
    chunks = -(-units // LANES)

    def marks(own):
        few = own.stop - own.start
        row = jnp.broadcast_to((tenants[...] + 1).astype(F32), (few, HOME))
        same = lax.broadcasted_iota(jnp.int32, (few, HOME), 0) + own.start
        same = same == lax.broadcasted_iota(jnp.int32, (few, HOME), 1)
        column = jnp.sum(jnp.where(same, row, 0.0), axis=1, keepdims=True)
        return jnp.broadcast_to(column, (few, 128))

    def tables_ready():
        device, rank = devices[...].astype(F32), rank_bins[...].astype(F32)
        n = device.shape[1]
        tenant = lax.broadcasted_iota(jnp.int32, (1, n), 1).astype(F32)
        same = lax.broadcasted_iota(jnp.int32, (n, n), 0) == lax.broadcasted_iota(
            jnp.int32, (n, n), 1
        )
        down_device = jnp.sum(jnp.where(same, device, 0.0), axis=1, keepdims=True)
        column = lax.broadcasted_iota(jnp.int32, (n, 128), 1)
        low = jnp.where(column < TP, x * TP + column, (column - TP) * TP).astype(F32)
        span = jnp.where(column < TP, 1, TP).astype(F32)
        places[...] = jnp.where(
            (down_device >= low) & (down_device < low + span), 1.0, 0.0
        ).astype(BF16)

        here = device == (x * TP + t).astype(F32)
        first = jnp.min(jnp.where(here, tenant, float(n)), axis=1, keepdims=True)
        second = jnp.max(jnp.where(here, tenant, -1.0), axis=1, keepdims=True)
        first_rank = jnp.sum(jnp.where(tenant == first, rank, 0.0), axis=1, keepdims=True)
        second_rank = jnp.sum(jnp.where(tenant == second, rank, 0.0), axis=1, keepdims=True)
        wide_shape = (1, gains.shape[1])
        span = lax.broadcasted_iota(jnp.int32, wide_shape, 1).astype(F32)
        gains[0:1, :] = jnp.where(span < first_rank, adapter_scale_fn / jnp.sqrt(first_rank), 0.0)
        gains[1:2, :] = jnp.where(
            (span >= first_rank) & (span < first_rank + second_rank),
            adapter_scale_fn / jnp.sqrt(second_rank),
            0.0,
        )
        gains[2:3, :] = jnp.broadcast_to(first + 1.0, wide_shape)
        gains[3:4, :] = jnp.broadcast_to(second + 1.0, wide_shape)

    def rows_ready():
        few = HOME // 2
        for k in range(2):
            own = slice(k * few, (k + 1) * few)

            for c in range(chunks):
                put_wide(
                    pl.ds(c + c // (PART - 1), few, stride=SLAB_ROWS),
                    columns(own, c * LANES, LANES),
                )
            for c in range(chunks + 1, SLAB_ROWS):
                put_wide(pl.ds(c, few, stride=SLAB_ROWS), jnp.zeros((few, LANES), F32))
            for j in range(LANES // 128):
                wide[j, pl.ds(PART - 1, few, stride=SLAB_ROWS), :] = marks(own)

            @pl.loop(0, few)
            def _(i):
                rows[k * few + i] = get_wide(pl.ds(i * SLAB_ROWS, SLAB_ROWS)).astype(BF16)

        rows[HOME] = jnp.zeros(rows.shape[1:], BF16)

    def a_copy(h, peer, slot):
        return remote(
            packed.at[pl.ds(peer * CAP, CAP), pl.ds(h * PART, PART)],
            groups[h].at[pl.ds(slot * CAP, CAP)],
            a_send.at[h, peer],
            a_recv.at[h, slot],
            (peer, t),
        )

    def a_own(h):
        return pltpu.make_async_copy(
            packed.at[pl.ds(x * CAP, CAP), pl.ds(h * PART, PART)],
            groups[h].at[pl.ds(x * CAP, CAP)],
            local_sem.at[4 + h],
        )

    def group_start():
        set_index(0, target(marks(slice(0, HOME)), TP, RING, CAP), HOME)

        @pl.loop(0, SLOTS)
        def _(i):
            packed[i] = rows[at_index(0, i, HOME + 1)]

        for h in range(2):
            others(RING, x, lambda peer: a_copy(h, peer, x).start())
            a_own(h).start()

    def t_copy(h, peer, slot):
        return remote(
            packed.at[pl.ds(peer * OWN, OWN), pl.ds(h * PART, PART)],
            owned.at[pl.ds(slot * OWN, OWN), pl.ds(h * PART, PART)],
            t_send.at[h, peer],
            t_recv.at[h, slot],
            (x, peer),
        )

    def t_own(h):
        return pltpu.make_async_copy(
            packed.at[pl.ds(t * OWN, OWN), pl.ds(h * PART, PART)],
            owned.at[pl.ds(t * OWN, OWN), pl.ds(h * PART, PART)],
            local_sem.at[6 + h],
        )

    def owner_start(h):
        a_own(h).wait()
        others(RING, x, lambda peer: a_copy(h, peer, peer).wait_recv())
        others(RING, x, lambda peer: a_copy(h, peer, peer).wait_send())

        if h == 0:

            @pl.loop(0, SLOTS)
            def _(i):
                wide[0, pl.ds(i * PART, PART), :] = groups[h][i, :, :128].astype(F32)

            mark = wide[0, pl.ds(PART - 1, SLOTS, stride=PART), :]
            set_index(2, target(mark, 0, TP, OWN), 0)

        @pl.loop(0, SLOTS)
        def _(i):
            packed[i, h * PART : (h + 1) * PART, :] = groups[h][at_index(2, i, SLOTS)]

        others(TP, t, lambda peer: t_copy(h, peer, t).start())
        t_own(h).start()

    def axes(p):
        return (y, z) if p == 0 else (z, y)

    def device(p, a, b):
        return (x, (b * RING + a if p == 0 else a * RING + b) * 2 + core)

    def partial_sum(p, a_to, column):
        b = axes(p)[1]
        total = None
        for k in range(2):
            left = []
            for i in range(RING):
                b_to = (b + i) % RING
                at = b_to * RING + a_to if p == 0 else a_to * RING + b_to
                left.append(xrecv[at, k * HOME : (k + 1) * HOME, :][:, :depth])
            term = jnp.dot(
                jnp.concatenate(left, axis=0),
                weight[k, :, pl.ds(column, TILE)],
                preferred_element_type=F32,
            )
            total = term if total is None else total + term
        return total

    def fill(p, slot, a_to, side, added=None):
        @pl.loop(0, half // TILE)
        def _(n):
            col = pl.multiple_of(n * TILE, TILE)
            total = partial_sum(p, a_to, pl.multiple_of((2 * p + side) * half + n * TILE, TILE))
            if added is not None:
                total = total + relay[p, added, :, pl.ds(col, TILE)].astype(F32)
            parts[p, slot, :, pl.ds(col, TILE)] = total.astype(BF16)

    def r_copy(p, k):
        a, b = axes(p)
        up_to, down_to = device(p, (a + 1) % RING, b), device(p, (a + 3) % RING, b)
        src, dst, to = [
            (0, relay.at[p, 0], up_to),
            (1, relay.at[p, 1], down_to),
            (2, fin_hbm.at[p, 1], up_to),
            (3, fin_hbm.at[p, 2], down_to),
            (0, fin_hbm.at[p, 0], up_to),
            (1, fin_hbm.at[p, 3], down_to),
        ][k]
        return remote(parts.at[p, src], dst, r_send.at[p, k], r_recv.at[p, k], to)

    def reduce_far(p, k):
        fill(p, k, (axes(p)[0] + 2) % RING, k)
        r_copy(p, k).start()

    def reduce_near(p, k):
        fill(p, 2 + k, (axes(p)[0] + 1 + 2 * k) % RING, 1 - k)
        r_copy(p, 2 + k).start()

    def reduce_pass(p, k):
        r_copy(p, k).wait()
        fill(p, k, (axes(p)[0] + 1 + 2 * k) % RING, k, added=k)
        r_copy(p, 4 + k).start()

    def down_copy(s):
        return pltpu.make_async_copy(
            down_in.at[:, pl.ds(pl.multiple_of(s * LANES, LANES), LANES)],
            down.at[s % AHEAD],
            down_sem.at[s % AHEAD],
        )

    tail = (chunks - 1) * LANES
    tail_copy = pltpu.make_async_copy(
        down_in.at[:, tail:units], down_tail, local_sem.at[24]
    )

    def up_copy(s):
        return pltpu.make_async_copy(
            up_in.at[:, pl.ds(pl.multiple_of(s * TILE, TILE), TILE)],
            up.at[s % UP_AHEAD],
            up_sem.at[s % UP_AHEAD],
        )

    def factors_start():
        for s in range(AHEAD):
            down_copy(s).start()
        for s in range(UP_AHEAD):
            up_copy(s).start()
        tail_copy.start()

    def latent_part(h):
        t_own(h).wait()
        others(TP, t, lambda peer: t_copy(h, peer, peer).wait_recv())

        @pl.loop(0, SLOTS)
        def _(i):
            put_wide(
                pl.ds(i * PART, PART), owned[i, h * PART : (h + 1) * PART, :].astype(F32)
            )

        first, last = h * (PART - 1), PART - 1 if h == 0 else chunks

        @pl.loop(0, last - first)
        def _(s):
            piece = get_wide(pl.ds(s, SLOTS, stride=PART)).astype(BF16)
            rows[pl.ds(s * OWN, OWN)] = piece.reshape(OWN, SLAB_ROWS, LANES)

        def term(s, factors):
            left = rows[pl.ds((s - first) * OWN, OWN)].reshape(SLOTS, LANES)
            left = left[:, : factors.shape[1]]
            return lax.dot_general(
                left, factors, (((1,), (1,)), ((), ())), preferred_element_type=F32
            )

        def step(s, total):
            down_copy(s).wait()
            total = total + term(s, down[s % AHEAD])

            @pl.when(s + AHEAD < chunks - 1)
            def _():
                down_copy(s + AHEAD).start()

            return total

        if h == 0:
            mark = get_wide(pl.ds(PART - 1, SLOTS, stride=PART))[:, : latents.shape[1]]
            gain[...] = jnp.where(mark == gains[2:3, :], gains[0:1, :], 0.0) + jnp.where(
                mark == gains[3:4, :], gains[1:2, :], 0.0
            )

        if h == 0:
            start = jnp.zeros(latents.shape, F32)
        else:
            tail_copy.wait()
            start = latents[...] + term(chunks - 1, down_tail[...])
        total = lax.fori_loop(first, min(last, chunks - 1), step, start)
        latents[...] = total if h == 0 else total * gain[...]

    def b_copy(h, peer, slot):
        return remote(
            packed.at[pl.ds(peer * OWN, OWN), pl.ds(h * PART, PART), pl.ds(0, OUT)],
            groups[h].at[pl.ds(slot * OWN, OWN), :, pl.ds(0, OUT)],
            b_send.at[h, peer],
            b_recv.at[h, slot],
            (x, peer),
        )

    def b_own(h):
        return pltpu.make_async_copy(
            packed.at[pl.ds(t * OWN, OWN), pl.ds(h * PART, PART), pl.ds(0, OUT)],
            groups[h].at[pl.ds(t * OWN, OWN), :, pl.ds(0, OUT)],
            local_sem.at[8 + h],
        )

    def back_start(h):
        steps = up_in.shape[1] // TILE
        left = latents[...].astype(BF16)
        others(TP, t, lambda peer: t_copy(h, peer, peer).wait_send())

        @pl.loop(h * steps // 2, (h + 1) * steps // 2)
        def _(s):
            up_copy(s).wait()
            product = jnp.dot(left, up[s % UP_AHEAD], preferred_element_type=F32)
            for j in range(TILE // OUT):
                put_wide(
                    pl.ds((s - h * (steps // 2)) * (TILE // OUT) + j, SLOTS, stride=PART),
                    product[:, j * OUT : (j + 1) * OUT],
                )

            @pl.when(s + UP_AHEAD < steps)
            def _():
                up_copy(s + UP_AHEAD).start()

        @pl.loop(0, SLOTS)
        def _(i):
            packed[i, h * PART : (h + 1) * PART, :OUT] = get_wide(
                pl.ds(i * PART, PART), OUT
            ).astype(BF16)

        others(TP, t, lambda peer: b_copy(h, peer, t).start())
        b_own(h).start()

    def s_copy(p, side, kind):
        a, b = axes(p)
        src, forward = [(1, True), (2 - 2 * side, False), (2 * side, True)][kind]
        step = 1 if forward == (side == 0) else 3
        return remote(
            second_out.at[p, side, src],
            second_in.at[p, side, kind],
            s_send.at[p, side, kind],
            s_recv.at[p, side, kind],
            device(p, a, (b + step) % RING),
        )

    def second_pass(p, side):
        s_copy(p, side, 0).wait()
        held = second_out.at[p, side, 2 * side]
        held[...] = (held[...].astype(F32) + second_in[p, side, 0].astype(F32)).astype(BF16)
        s_copy(p, side, 2).start()

    def stage_copy(p, slot):
        return pltpu.make_async_copy(
            fin_hbm.at[p, slot], parts.at[p, slot], local_sem.at[16 + 4 * p + slot]
        )

    def reduce_stage(p, side):
        for k in (4, 3) if side == 0 else (2, 5):
            r_copy(p, k).wait_recv()
        for k in (4 + side, 2 + side):
            r_copy(p, k).wait_send()
        for i in range(2):
            stage_copy(p, side + 2 * i).start()

    def reduce_second(p, side):
        for i in range(2):
            stage_copy(p, side + 2 * i).wait()

        @pl.loop(0, half // TILE)
        def _(n):
            col = pl.multiple_of(n * TILE, TILE)
            at = pl.multiple_of(side * half + n * TILE, TILE)
            total = partial_sum(
                p, axes(p)[0], pl.multiple_of((2 * p + side) * half + n * TILE, TILE)
            )
            total = total + parts[p, side, :, pl.ds(col, TILE)].astype(F32)
            total = total + parts[p, 2 + side, :, pl.ds(col, TILE)].astype(F32)
            own_sum[p, :, pl.ds(at, TILE)] = total[:HOME]
            for d in range(1, RING):
                second_out[p, side, d - 1, :, pl.ds(col, TILE)] = total[
                    d * HOME : (d + 1) * HOME
                ].astype(BF16)

        for kind in range(2):
            s_copy(p, side, kind).start()

    def c_copy(h, peer, slot):
        return remote(
            packed.at[pl.ds(peer * CAP, CAP), pl.ds(h * PART, PART), pl.ds(OUT, OUT)],
            home_in.at[pl.ds(slot * CAP, CAP), pl.ds(h * PART, PART)],
            c_send.at[h, peer],
            c_recv.at[h, slot],
            (peer, t),
        )

    def c_own(h):
        return pltpu.make_async_copy(
            packed.at[pl.ds(x * CAP, CAP), pl.ds(h * PART, PART), pl.ds(OUT, OUT)],
            home_in.at[pl.ds(x * CAP, CAP), pl.ds(h * PART, PART)],
            local_sem.at[10 + h],
        )

    def home_start(h):
        b_own(h).wait()
        others(TP, t, lambda peer: b_copy(h, peer, peer).wait_recv())

        @pl.loop(0, SLOTS)
        def _(i):
            packed[i, h * PART : (h + 1) * PART, OUT:] = groups[h][at_index(3, i, SLOTS)][:, :OUT]

        others(RING, x, lambda peer: c_copy(h, peer, x).start())
        c_own(h).start()

    def second_arrived():
        for p in range(2):
            for side in range(2):
                for kind in range(1, 3):
                    s_copy(p, side, kind).wait()

                @pl.loop(0, half // TILE)
                def _(n):
                    at = pl.ds(pl.multiple_of(n * TILE, TILE), TILE)
                    column = pl.ds(pl.multiple_of(side * half + n * TILE, TILE), TILE)
                    total = own_sum[p, :, column]
                    for kind in range(1, 3):
                        total = total + second_in[p, side, kind, :, at].astype(F32)
                    own_sum[p, :, column] = total

    def home_arrived(h):
        c_own(h).wait()
        others(RING, x, lambda peer: c_copy(h, peer, peer).wait_recv())

    def finish():
        few = HOME // 2
        for k in range(2):
            own = slice(k * few, (k + 1) * few)

            @pl.loop(0, few)
            def _(i):
                put_wide(pl.ds(i * SLAB_ROWS, SLAB_ROWS), home_in[at_index(1, k * few + i, SLOTS)].astype(F32))

            @pl.loop(0, SLAB_ROWS)
            def _(n):
                column = pl.multiple_of(n * OUT, OUT)
                at = pl.ds(pl.multiple_of(n % PART * OUT, OUT), OUT)
                total = own_sum[n // PART, own, at]
                total = total + get_wide(pl.ds(n, few, stride=SLAB_ROWS), OUT)
                out[own, pl.ds(column, OUT)] = total.astype(BF16)

    def all_left():
        others(CHIPS, chip, lambda peer: x_copy(peer, peer).wait_send())
        for h in range(2):
            others(TP, t, lambda peer: b_copy(h, peer, peer).wait_send())
            others(RING, x, lambda peer: c_copy(h, peer, peer).wait_send())

    base_start()
    factors_start()
    tables_ready()
    rows_ready()
    group_start()
    owner_start(0)
    base_arrived()
    reduce_far(0, 0)
    reduce_far(1, 0)
    reduce_far(0, 1)
    reduce_far(1, 1)
    reduce_near(0, 0)
    reduce_near(1, 0)
    owner_start(1)
    reduce_near(0, 1)
    reduce_near(1, 1)
    reduce_pass(0, 0)
    reduce_pass(1, 0)
    latent_part(0)
    reduce_pass(0, 1)
    reduce_pass(1, 1)
    latent_part(1)
    back_start(0)
    back_start(1)
    reduce_stage(0, 0)
    reduce_stage(1, 0)
    reduce_second(0, 0)
    reduce_stage(0, 1)
    reduce_second(1, 0)
    reduce_stage(1, 1)
    reduce_second(0, 1)
    reduce_second(1, 1)
    home_start(0)
    second_pass(0, 0)
    second_pass(1, 0)
    home_start(1)
    second_pass(0, 1)
    second_pass(1, 1)
    second_arrived()
    home_arrived(0)
    home_arrived(1)
    finish()
    all_left()


def local(
    hidden,
    draft_row_client,
    client_rank_bin,
    client_device,
    down_weight,
    packed_down_factors,
    packed_up_factors,
):
    depth, width = down_weight.shape
    units, rank_columns = packed_down_factors.shape
    tenants = client_rank_bin.shape[0]

    vmem, hbm = pl.BlockSpec(memory_space=pltpu.VMEM), pl.BlockSpec(memory_space=pl.ANY)
    dma = pltpu.SemaphoreType.DMA
    half = width // 4
    out, _ = pl.pallas_call(
        body,
        out_shape=(
            jax.ShapeDtypeStruct((HOME, width), BF16),
            jax.ShapeDtypeStruct((2, 4, RING * HOME, half), BF16),
        ),
        in_specs=[vmem, vmem, vmem, vmem, hbm, hbm, hbm],
        out_specs=(vmem, hbm),
        scratch_shapes=[
            pltpu.VMEM((CHIPS, 2 * HOME, LANES), BF16),
            pltpu.VMEM((HOME + 1, SLAB_ROWS, LANES), BF16),
            pltpu.VMEM((CHIPS, 2 * HOME, LANES), BF16),
            pltpu.VMEM((2, depth, width), BF16),
            pltpu.VMEM((SLOTS, SLAB_ROWS, LANES), BF16),
            pltpu.VMEM((SLOTS, PART, LANES), BF16),
            pltpu.VMEM((SLOTS, PART, LANES), BF16),
            pltpu.VMEM((SLOTS, SLAB_ROWS, LANES), BF16),
            pltpu.VMEM((LANES // 128, SLOTS * PART, 128), F32),
            pltpu.VMEM((AHEAD, rank_columns, LANES), BF16),
            pltpu.VMEM((rank_columns, units % LANES), BF16),
            pltpu.VMEM((UP_AHEAD, rank_columns, TILE), BF16),
            pltpu.VMEM((SLOTS, SLAB_ROWS, OUT), BF16),
            pltpu.VMEM((2, 4, RING * HOME, half), BF16),
            pltpu.VMEM((2, 2, RING * HOME, half), BF16),
            pltpu.VMEM((2, 2, 3, HOME, half), BF16),
            pltpu.VMEM((2, 2, 3, HOME, half), BF16),
            pltpu.VMEM((2, HOME, 2 * half), F32),
            pltpu.VMEM((SLOTS, rank_columns), F32),
            pltpu.VMEM((SLOTS, rank_columns), F32),
            pltpu.VMEM((tenants, 128), BF16),
            pltpu.VMEM((8, rank_columns), F32),
            pltpu.VMEM((4, 8, 128), jnp.int32),
            pltpu.SMEM((4, 8, 128), jnp.int32),
            dma((25,)),
            dma((AHEAD,)),
            dma((UP_AHEAD,)),
            dma((2,)),
            dma((CHIPS,)),
            dma((CHIPS,)),
            dma((2, RING)),
            dma((2, RING)),
            dma((2, TP)),
            dma((2, TP)),
            dma((2, TP)),
            dma((2, TP)),
            dma((2, RING)),
            dma((2, RING)),
            dma((2, 6)),
            dma((2, 6)),
            dma((2, 2, 3)),
            dma((2, 2, 3)),
        ],
        compiler_params=pltpu.CompilerParams(
            collective_id=0, has_side_effects=True, vmem_limit_bytes=63 << 20
        ),
        name="verify_rows",
    )(
        draft_row_client.reshape(1, HOME),
        client_rank_bin.reshape(1, tenants),
        client_device.reshape(1, tenants),
        hidden,
        down_weight,
        packed_down_factors.T,
        packed_up_factors,
    )
    return out


def solution(mesh):
    placed = (
        P(("dp", "tp"), None),
        P(("dp", "tp")),
        P(),
        P(),
        P("tp", None),
        P(None, ("dp", "tp")),
        P(("dp", "tp"), None),
    )
    return jax.shard_map(
        local, mesh=mesh, in_specs=placed, out_specs=P(("dp", "tp"), None), check_vma=False
    )
```
